128 devices in a mesh: stretch: 32 (over x, z, core), space: 4 (over y).
Axes of the slice: x: 4, y: 4, z: 4, core: 2. Of those that a mesh axis runs over, the one named last changes fastest.
Arguments:
- frames: bfloat16 [128, 8, 32, 384], P('stretch', 'space')
- stretch_table: int32 [32, 4], P('stretch'), may hold values from -1 to 31, as said below
- conv_weight: bfloat16 [2, 3, 3, 3, 384, 384], replicated, may hold values from -0.0625 to 0.0625
- norm_gain: float32 [2, 384], replicated, may hold values from 0.5 to 1.5
- norm_bias: float32 [2, 384], replicated, may hold values from -3 to 3
- cotangent: bfloat16 [128, 8, 32, 384], P('stretch', 'space'), may hold values from -6 to 6
Outputs:
- block_output: bfloat16 [128, 8, 32, 384], P('stretch', 'space')
- input_grad: bfloat16 [128, 8, 32, 384], P('stretch', 'space')
The draws below stay inside these ranges and needn't reach their ends.
Inputs may be any that keep to these rules, and one draw needn't show every extreme that they name: `stretch_table`: row d describes the stretch held at index d of the stretch axis: its clip's number, its position in the clip (0 at a clip's first stretch), the index that holds the clip's next stretch and the one that holds its previous stretch, -1 where there is none. A stretch's successor names it as its predecessor.
All inputs are finite; a program needn't handle non-finite values.
Results may differ from the reference program's by a relative error of at most 0.015.
Values may be sent and summed in bfloat16 or wider, within the bound.
No kernel may reach another device: no remote copies, remote signals or barrier semaphores. Data moves between devices by JAX's collectives and lax.ppermute only.
A program may use at most 128 MiB of HBM per device.

```python
import math
import jax
import jax.numpy as jnp
from jax import lax

C = 384
GROUPS = 32
FRAMES = 4
LAYERS = 2
COLS = 32
NCHUNK = 32
ROWS = 8


def draw_frames(key, part):
    key = jax.random.fold_in(key, 5)
    keys = jax.random.split(key, 4)
    full_shape = (NCHUNK * FRAMES, ROWS, COLS, C)
    row_scale = jnp.exp(jax.random.uniform(keys[0], (NCHUNK * FRAMES, ROWS, 1, 1)) * math.log(10.0))
    col_scale = jnp.exp(jax.random.uniform(keys[1], (1, 1, COLS, 1)) * math.log(10.0))
    chan_scale = jnp.exp(jax.random.uniform(keys[2], (1, 1, 1, C)) * math.log(10.0))
    base = jnp.clip(jax.random.normal(keys[3], full_shape), -4.0, 4.0)
    return (base * row_scale * col_scale * chan_scale * 0.03).astype(jnp.bfloat16)


def draw_stretch_table(key, part):
    key = jax.random.fold_in(key, 11)
    keys = jax.random.split(key, 2)
    index = jnp.arange(NCHUNK, dtype=jnp.int32)
    starts = (jax.random.randint(keys[0], (NCHUNK,), 0, 4) == 0) | (index == 0)
    starts = starts.astype(jnp.int32)
    first_of_clip = lax.cummax(jnp.where(starts > 0, index, 0), axis=0)
    clip_number = jnp.cumsum(starts) - 1
    position = index - first_of_clip
    holder = jax.random.permutation(keys[1], NCHUNK).astype(jnp.int32)
    before = jnp.maximum(index - 1, 0)
    after = jnp.minimum(index + 1, NCHUNK - 1)
    source_dev = jnp.where(position > 0, holder[before], -1)
    follows = (index + 1 < NCHUNK) & (position[after] > 0)
    target_dev = jnp.where(follows, holder[after], -1)
    described = jnp.stack([clip_number, position, target_dev, source_dev], axis=1).astype(jnp.int32)
    return jnp.zeros((NCHUNK, 4), jnp.int32).at[holder].set(described)


def levels(stream_key, dims, pieces, least, largest):
    loudness, own = 1.0, jax.random.fold_in(stream_key, 6)
    for dim, parts in pieces:
        heights = jnp.exp(jax.random.uniform(jax.random.fold_in(own, dim), (parts,), jnp.float32, least / len(pieces), largest / len(pieces)))
        loudness = loudness * jnp.repeat(heights, dims[dim] // parts).reshape([-1 if axis == dim else 1 for axis in range(len(dims))])
    return loudness


def gaussian(stream_key, shape, deviation, limit, shards=(), kind=jnp.bfloat16):
    level = levels(stream_key, shape, shards, -0.22, 0.18) if shards else 1.0
    entries = jax.random.normal(stream_key, shape, jnp.float32) * deviation * level
    return jnp.minimum(jnp.maximum(entries, -limit), limit).astype(kind)


def setup_inputs(seed: int = 0) -> dict:
    key_list = jax.random.split(jax.random.key(seed), 7)
    return {
        "frames": draw_frames(jax.random.fold_in(key_list[6], 71), 0),
        "stretch_table": draw_stretch_table(jax.random.fold_in(key_list[6], 71), 0),
        "conv_weight": gaussian(key_list[2], (LAYERS, 3, 3, 3, C, C), (27 * C) ** -0.5, 0.0625),
        "norm_gain": jnp.clip(jax.random.uniform(key_list[3], (LAYERS, C), jnp.float32, 0.5, 1.5), 0.5, 1.5),
        "norm_bias": gaussian(key_list[4], (LAYERS, C), 0.5, 3.0, (), jnp.float32),
        "cotangent": gaussian(key_list[5], (NCHUNK * FRAMES, ROWS, COLS, C), 1.0, 6.0, ((0, 32), (1, 4))),
    }


def norm_silu(acts, gain_row, bias_row):
    nchunk, nframe, nrow, ncol, nchan = acts.shape
    grouped = acts.reshape(nchunk, nframe, nrow, ncol, GROUPS, nchan // GROUPS)
    mean_val = lax.optimization_barrier(jnp.mean(grouped, axis=(2, 3, 5), keepdims=True))
    centered = grouped - mean_val
    variance = lax.optimization_barrier(jnp.mean(centered * centered, axis=(2, 3, 5), keepdims=True))
    normed = (centered * lax.rsqrt(variance + 1e-05)).reshape(acts.shape)
    return jax.nn.silu(normed * gain_row + bias_row)

def convolve(extended, weight_f32):
    padded = jnp.pad(extended, ((0, 0), (0, 0), (1, 1), (1, 1), (0, 0)))
    return lax.conv_general_dilated(padded, weight_f32, (1, 1, 1), 'VALID', dimension_numbers=('NDHWC', 'DHWIO', 'NDHWC'), precision=lax.Precision.HIGHEST)

def reference(frames, stretch_table, conv_weight, norm_gain, norm_bias, cotangent):
    acts = frames.reshape(NCHUNK, FRAMES, ROWS, COLS, C)
    source_dev = stretch_table[:, 3]
    target_dev = stretch_table[:, 2]
    has_source = (source_dev >= 0)[:, None, None, None, None]
    has_target = (target_dev >= 0)[:, None, None, None, None]
    source_safe = jnp.where(source_dev >= 0, source_dev, 0).astype(jnp.int32)
    target_safe = jnp.where(target_dev >= 0, target_dev, 0).astype(jnp.int32)
    saved = []
    for layer_idx in range(LAYERS):
        acts_f32 = acts.astype(jnp.float32)
        saved.append(acts_f32)
        normed = norm_silu(acts_f32, norm_gain[layer_idx], norm_bias[layer_idx]).astype(jnp.bfloat16)
        carried = jnp.where(has_source, normed[source_safe, FRAMES - 2:], jnp.zeros((), jnp.bfloat16))
        extended = jnp.concatenate([carried, normed], axis=1).astype(jnp.float32)
        weight_f32 = conv_weight[layer_idx].astype(jnp.float32)
        acts = convolve(extended, weight_f32).astype(jnp.bfloat16)
    block_output = acts.reshape(frames.shape)
    grad_acts = cotangent.reshape(NCHUNK, FRAMES, ROWS, COLS, C)
    for layer_idx in reversed(range(LAYERS)):
        weight_f32 = conv_weight[layer_idx].astype(jnp.float32)
        primal = jnp.zeros((NCHUNK, FRAMES + 2, ROWS, COLS, C), jnp.float32)
        unused, pull_conv = jax.vjp(lambda ext_in: convolve(ext_in, weight_f32), primal)
        ext_grad = pull_conv(grad_acts.astype(jnp.float32))[0]
        returned = jnp.where(has_target, ext_grad[target_safe, :2], jnp.zeros((), jnp.float32))
        norm_grad = ext_grad[:, 2:].at[:, FRAMES - 2:].add(returned)
        gain_row = norm_gain[layer_idx]
        bias_row = norm_bias[layer_idx]
        unused, pull_norm = jax.vjp(lambda acts_in: norm_silu(acts_in, gain_row, bias_row), saved[layer_idx])
        grad_acts = pull_norm(norm_grad)[0].astype(jnp.bfloat16)
    return (block_output, grad_acts.reshape(frames.shape))
```

```python
import jax
import jax.numpy as jnp
from jax import lax
from jax.experimental import pallas as pl
from jax.experimental.pallas import tpu as pltpu
from jax.sharding import PartitionSpec as P

C = 384
GROUPS = 32
GSIZE = C // GROUPS
COLS = 32
ROWS = 8
CELLS = ROWS * COLS
PADDED = CELLS + 2 * COLS
COUNT = float(CELLS * GSIZE)
F32 = jnp.float32
BF16 = jnp.bfloat16
VMEM = pl.BlockSpec(memory_space=pltpu.VMEM)
SMEM = pl.BlockSpec(memory_space=pltpu.SMEM)
ANY = pl.BlockSpec(memory_space=pl.ANY)


def group_matrix():
    row = lax.broadcasted_iota(jnp.int32, (C, C), 0) // GSIZE
    col = lax.broadcasted_iota(jnp.int32, (C, C), 1) // GSIZE
    return (row == col).astype(BF16)


def group_mean(sums, ones):
    n = sums.shape[0]
    high = sums.astype(BF16)
    rest = sums - high.astype(F32)
    mid = rest.astype(BF16)
    low = (rest - mid.astype(F32)).astype(BF16)
    parts = jnp.dot(
        jnp.concatenate([high.astype(F32), mid.astype(F32), low.astype(F32)], axis=0).astype(BF16),
        ones[...],
        preferred_element_type=F32,
    )
    return (parts[:n] + parts[n : 2 * n] + parts[2 * n :]) * (1.0 / COUNT)


def fold(values):
    return jnp.sum(values.reshape(COLS // 8, 8, C), axis=0)


def sigmoid(v):
    return 0.5 * jnp.tanh(0.5 * v) + 0.5


def store_shifted(slab, idx, row, values):
    col = lax.broadcasted_iota(jnp.int32, (COLS, C), 0)
    left = jnp.where(col == 0, 0.0, pltpu.roll(values, 1, 0))
    right = jnp.where(col == COLS - 1, 0.0, pltpu.roll(values, COLS - 1, 0))
    at = pl.ds(row * COLS, COLS)
    slab[idx, at, 0:C] = left.astype(BF16)
    slab[idx, at, C : 2 * C] = values.astype(BF16)
    slab[idx, at, 2 * C : 3 * C] = right.astype(BF16)


def conv_tap(slab_in, taps, a, acc, f):
    w = jnp.concatenate(
        [taps[pl.ds(a * 9 + 3 * b, 3)].reshape(3 * C, C) for b in range(3)], axis=1
    )
    y = jnp.dot(slab_in, w, preferred_element_type=F32)
    for b in range(3):
        acc[f, (2 - b) * COLS : (2 - b) * COLS + CELLS, :] += y[:, b * C : (b + 1) * C]


def adjoint_tap(slab_in, taps, a, acc, f):
    w = jnp.concatenate(
        [
            jnp.concatenate([taps[a * 9 + 3 * b + 2 - e] for e in range(3)], axis=1)
            for b in range(3)
        ],
        axis=0,
    )
    y = lax.dot_general(slab_in, w, (((1,), (1,)), ((), ())), preferred_element_type=F32)
    for b in range(3):
        acc[f, b * COLS : b * COLS + CELLS, :] += y[:, b * C : (b + 1) * C]


def frame_sums(x, idx):
    def body(r, tot):
        return tot + fold(x[idx, pl.ds(r * COLS, COLS), :].astype(F32))

    tot = lax.fori_loop(0, ROWS, body, jnp.zeros((8, C), F32), unroll=True)
    return jnp.sum(tot, axis=0, keepdims=True)


def frame_square_sums(x, idx, mean):
    def body(r, tot):
        diff = x[idx, pl.ds(r * COLS, COLS), :].astype(F32) - mean
        return tot + fold(diff * diff)

    tot = lax.fori_loop(0, ROWS, body, jnp.zeros((8, C), F32), unroll=True)
    return jnp.sum(tot, axis=0, keepdims=True)


def frame_stats(x, count, sums, mean, inv_std, ones):
    sums[...] = jnp.zeros_like(sums)

    def total(n, _):
        sums[pl.ds(n, 1), :] = frame_sums(x, n)
        return 0

    lax.fori_loop(0, count, total, 0)
    mean[...] = group_mean(sums[...], ones)

    def square(n, _):
        sums[pl.ds(n, 1), :] = frame_square_sums(x, n, mean[pl.ds(n, 1), :])
        return 0

    lax.fori_loop(0, count, square, 0)
    inv_std[...] = lax.rsqrt(group_mean(sums[...], ones) + 1e-5)


def norm_silu_frame(x, idx, mean, inv_std, gain, bias, slab, out_idx, mask):
    scale = inv_std * gain

    def body(r, _):
        v = (x[idx, pl.ds(r * COLS, COLS), :].astype(F32) - mean) * scale + bias
        s = v * sigmoid(v)
        if mask is not None:
            s = s * mask
        store_shifted(slab, out_idx, r, s)
        return 0

    lax.fori_loop(0, ROWS, body, 0, unroll=2)


def norm_back_sums(x, idx, mean, inv_std, gain, bias, acc, f):
    def body(r, tot):
        at = pl.ds(COLS + r * COLS, COLS)
        n = (x[idx, pl.ds(r * COLS, COLS), :].astype(F32) - mean) * inv_std
        v = n * gain + bias
        sig = sigmoid(v)
        gn = acc[f, at, :] * (sig * (1.0 + v * (1.0 - sig)) * gain)
        acc[f, at, :] = gn
        return tot[0] + fold(gn), tot[1] + fold(gn * n)

    zero = jnp.zeros((8, C), F32)
    one, two = lax.fori_loop(0, ROWS, body, (zero, zero), unroll=2)
    return jnp.sum(one, axis=0, keepdims=True), jnp.sum(two, axis=0, keepdims=True)


def norm_back_row(x, idx, r, mean, inv_std, acc, f, first, second):
    n = (x[idx, pl.ds(r * COLS, COLS), :].astype(F32) - mean) * inv_std
    return inv_std * (acc[f, pl.ds(COLS + r * COLS, COLS), :] - first - n * second)


def read_row(block):
    parts = [block(cb).astype(F32) for cb in range(4)]
    raw = jnp.concatenate([p[:8] for p in parts], axis=0)
    cot = jnp.concatenate([p[8:] for p in parts], axis=0)
    return raw, cot


def start_weights(weight, taps, sems):
    for layer in range(2):
        for a in range(3):
            pltpu.make_async_copy(
                weight.at[layer, pl.ds(a * 9, 9)],
                taps.at[layer, pl.ds(a * 9, 9)],
                sems.at[layer, a],
            ).start()


def wait_weights(weight, taps, sems, layer):
    for a in range(3):
        pltpu.make_async_copy(
            weight.at[layer, pl.ds(a * 9, 9)], taps.at[layer, pl.ds(a * 9, 9)], sems.at[layer, a]
        ).wait()


def route_kernel(place, table, pieces, out):
    g = place[0] // 8

    def body(d, _):
        nxt, prv = table[d, 2], table[d, 3]
        for j in range(4):
            src = jnp.where(j <= g, prv, jnp.where(j >= g + 2, nxt, -1))
            cot_src = jnp.where(j >= g, nxt, -1)
            raw = pieces[jnp.maximum(src, 0)].astype(F32)[:8]
            cot = pieces[jnp.maximum(cot_src, 0)].astype(F32)[8:]
            raw = raw * (src >= 0).astype(F32)
            cot = cot * (cot_src >= 0).astype(F32)
            out[d * 4 + j] = jnp.concatenate([raw, cot], axis=0).astype(BF16)
        return 0

    lax.fori_loop(0, 32, body, 0)


def own_kernel(
    place, mine, from1, from2, from3, gain, bias, weight, acc0, acc1,
    taps, x, slab, gslab, sums, mean, inv_std, ones, sems,
):
    start_weights(weight, taps, sems)
    j = place[1]
    ones[...] = group_matrix()
    acc0[...] = jnp.zeros_like(acc0)
    acc1[...] = jnp.zeros_like(acc1)
    for shift, part in enumerate((mine, from1, from2, from3)):
        holder = lax.rem(j + 4 - shift, 4)

        def rows(t, _, part=part, holder=holder):
            g, r = t // 2, lax.rem(t, 2)
            raw, cot = read_row(lambda cb: part[t * 4 + cb])
            x[g, pl.ds((holder * 2 + r) * COLS, COLS), :] = raw.astype(BF16)
            store_shifted(gslab, g, holder * 2 + r, cot)
            return 0

        lax.fori_loop(0, 8, rows, 0)
    frame_stats(x, 4, sums, mean, inv_std, ones)

    def normed(g, _):
        norm_silu_frame(
            x, g, mean[pl.ds(g, 1), :], inv_std[pl.ds(g, 1), :],
            gain[0:1, :], bias[0:1, :], slab, g, None,
        )
        return 0

    lax.fori_loop(0, 4, normed, 0)
    wait_weights(weight, taps, sems, 0)

    def forward(t, _):
        g, a = t // 3, lax.rem(t, 3)
        f = g + 4 - j - a

        @pl.when((f >= 0) & (f <= 4))
        def _():
            conv_tap(slab[g], taps.at[0], a, acc0, f)

        return 0

    lax.fori_loop(0, 12, forward, 0)
    wait_weights(weight, taps, sems, 1)

    def backward(t, _):
        g, a = t // 3, lax.rem(t, 3)
        u = g - j
        f = u - 2 + a

        @pl.when((u >= 0) & (f >= 0) & (f <= 2))
        def _():
            adjoint_tap(gslab[g], taps.at[1], a, acc1, f)

        return 0

    lax.fori_loop(0, 12, backward, 0)


def rest_kernel(
    place, mine, from1, from2, from3, recv, acc0_in, acc1_in, gain, bias, weight, out,
    taps, x, slab, gslab, acc0, acc1, acc2, h, sums, mean, inv_std, ones, raw_own, sems,
):
    start_weights(weight, taps, sems)
    j = place[1]
    has_prev = (place[2] >= 0).astype(F32)
    ones[...] = group_matrix()
    acc0[...] = acc0_in[...]
    acc1[...] = acc1_in[...]

    for shift, part in enumerate((mine, from1, from2, from3)):
        holder = lax.rem(j + 4 - shift, 4)
        for r in range(2):
            raw, _ = read_row(lambda cb: part[(j * 2 + r) * 4 + cb])
            raw_own[0, pl.ds((holder * 2 + r) * COLS, COLS), :] = raw.astype(BF16)

    def rows(t, _):
        g, row = t // 8, lax.rem(t, 8)
        i, r = row // 2, lax.rem(row, 2)
        raw, cot = read_row(lambda cb: recv[((g * 2 + r) * 4 + cb) * 4 + i])
        x[g, pl.ds(row * COLS, COLS), :] = raw.astype(BF16)
        store_shifted(gslab, g, row, cot)
        return 0

    lax.fori_loop(0, 32, rows, 0)
    frame_stats(x, 4, sums, mean, inv_std, ones)

    def normed(g, _):
        mask = jnp.where(g >= j, has_prev, 1.0)
        norm_silu_frame(
            x, g, mean[pl.ds(g, 1), :], inv_std[pl.ds(g, 1), :],
            gain[0:1, :], bias[0:1, :], slab, g, mask,
        )
        return 0

    lax.fori_loop(0, 4, normed, 0)
    wait_weights(weight, taps, sems, 0)

    def forward(t, _):
        g, a = t // 3, lax.rem(t, 3)
        w = jnp.where(g >= j, g - j, g - j + 8)
        f = w - a

        @pl.when((f >= 0) & (f <= 4) & (g != j - 1))
        def _():
            conv_tap(slab[g], taps.at[0], a, acc0, f)

        return 0

    lax.fori_loop(0, 12, forward, 0)
    wait_weights(weight, taps, sems, 1)

    def backward(t, _):
        g, a = t // 3, lax.rem(t, 3)
        u = g + 4 - j
        f = u - 2 + a

        @pl.when((u <= 4) & (f >= 0) & (f <= 2))
        def _():
            adjoint_tap(gslab[g], taps.at[1], a, acc1, f)

        return 0

    lax.fori_loop(0, 12, backward, 0)

    def rounded(f, _):
        h[f] = acc0[f, COLS : COLS + CELLS, :].astype(BF16)
        return 0

    lax.fori_loop(0, 5, rounded, 0)
    frame_stats(h, 5, sums, mean, inv_std, ones)
    gain1, bias1 = gain[1:2, :], bias[1:2, :]

    def normed1(f, _):
        mask = jnp.where(j - 2 + f < 0, has_prev, 1.0)
        norm_silu_frame(
            h, f, mean[pl.ds(f, 1), :], inv_std[pl.ds(f, 1), :], gain1, bias1, slab, f, mask
        )
        return 0

    lax.fori_loop(0, 3, normed1, 0)
    acc2[...] = jnp.zeros_like(acc2)

    def last(a, _):
        conv_tap(slab[a], taps.at[1], a, acc2, 0)
        return 0

    lax.fori_loop(0, 3, last, 0)
    for i in range(4):
        out[i, 0] = acc2[0, COLS + i * 64 : COLS + i * 64 + 64, :].astype(BF16)

    sums[...] = jnp.zeros_like(sums)

    def back_sums(f, _):
        n = f + 2
        one, two = norm_back_sums(
            h, n, mean[pl.ds(n, 1), :], inv_std[pl.ds(n, 1), :], gain1, bias1, acc1, f
        )
        sums[pl.ds(f, 1), :] = one
        sums[pl.ds(f + 4, 1), :] = two
        return 0

    lax.fori_loop(0, 3, back_sums, 0)
    sums[...] = group_mean(sums[...], ones)

    def back_rows(t, _):
        f, r = t // 8, lax.rem(t, 8)
        n = f + 2
        g1 = norm_back_row(
            h, n, r, mean[pl.ds(n, 1), :], inv_std[pl.ds(n, 1), :], acc1, f,
            sums[pl.ds(f, 1), :], sums[pl.ds(f + 4, 1), :],
        )
        store_shifted(slab, f, r, g1)
        return 0

    lax.fori_loop(0, 24, back_rows, 0)
    acc2[...] = jnp.zeros_like(acc2)

    def first(a, _):
        adjoint_tap(slab[2 - a], taps.at[0], a, acc2, 0)
        return 0

    lax.fori_loop(0, 3, first, 0)

    frame_stats(raw_own, 1, sums, mean, inv_std, ones)
    m0, i0 = mean[0:1, :], inv_std[0:1, :]
    one, two = norm_back_sums(raw_own, 0, m0, i0, gain[0:1, :], bias[0:1, :], acc2, 0)
    sums[0:1, :] = one
    sums[1:2, :] = two
    sums[...] = group_mean(sums[...], ones)
    for r in range(8):
        g0 = norm_back_row(raw_own, 0, r, m0, i0, acc2, 0, sums[0:1, :], sums[1:2, :])
        out[r // 2, 1, (r % 2) * COLS : (r % 2 + 1) * COLS, :] = g0.astype(BF16)


def per_device(frames, stretch_table, conv_weight, norm_gain, norm_bias, cotangent):
    params = pltpu.CompilerParams(vmem_limit_bytes=58 * 2**20)
    stretch, space = lax.axis_index("stretch"), lax.axis_index("space")
    place = jnp.stack([stretch, space, stretch_table[0, 3], stretch_table[0, 2]]).astype(jnp.int32)
    pieces = jnp.concatenate([frames.reshape(32, 8, C), cotangent.reshape(32, 8, C)], axis=1)
    weight = conv_weight.reshape(2, 27, C, C)
    table = lax.all_gather(stretch_table, "stretch", axis=0, tiled=True)
    spread = lax.all_to_all(pieces, "stretch", 0, 0, tiled=True)
    shifted = [
        lax.ppermute(pieces, "space", [(i, (i + k) % 4) for i in range(4)]) for k in (1, 2, 3)
    ]
    routed = pl.pallas_call(
        route_kernel,
        out_shape=jax.ShapeDtypeStruct((128, 16, C), BF16),
        in_specs=[SMEM, SMEM, VMEM],
        out_specs=VMEM,
        name="route",
    )(place, table, spread)
    recv = lax.all_to_all(routed, ("stretch", "space"), 0, 0, tiled=True)
    acc0, acc1 = pl.pallas_call(
        own_kernel,
        out_shape=[
            jax.ShapeDtypeStruct((5, PADDED, C), F32),
            jax.ShapeDtypeStruct((3, PADDED, C), F32),
        ],
        in_specs=[SMEM, VMEM, VMEM, VMEM, VMEM, VMEM, VMEM, ANY],
        out_specs=[VMEM, VMEM],
        scratch_shapes=[
            pltpu.VMEM((2, 27, C, C), BF16),
            pltpu.VMEM((4, CELLS, C), BF16),
            pltpu.VMEM((4, CELLS, 3 * C), BF16),
            pltpu.VMEM((4, CELLS, 3 * C), BF16),
            pltpu.VMEM((8, C), F32),
            pltpu.VMEM((8, C), F32),
            pltpu.VMEM((8, C), F32),
            pltpu.VMEM((C, C), BF16),
            pltpu.SemaphoreType.DMA((2, 3)),
        ],
        compiler_params=params,
        cost_estimate=pl.CostEstimate(
            flops=15 * 2 * CELLS * 9 * C * C, bytes_accessed=24 * 2**20, transcendentals=0
        ),
        name="own",
    )(place, pieces, *shifted, norm_gain, norm_bias, weight)
    out = pl.pallas_call(
        rest_kernel,
        out_shape=jax.ShapeDtypeStruct((4, 2, 64, C), BF16),
        in_specs=[SMEM, VMEM, VMEM, VMEM, VMEM, VMEM, VMEM, VMEM, VMEM, VMEM, ANY],
        out_specs=VMEM,
        scratch_shapes=[
            pltpu.VMEM((2, 27, C, C), BF16),
            pltpu.VMEM((4, CELLS, C), BF16),
            pltpu.VMEM((4, CELLS, 3 * C), BF16),
            pltpu.VMEM((4, CELLS, 3 * C), BF16),
            pltpu.VMEM((5, PADDED, C), F32),
            pltpu.VMEM((3, PADDED, C), F32),
            pltpu.VMEM((1, PADDED, C), F32),
            pltpu.VMEM((5, CELLS, C), BF16),
            pltpu.VMEM((8, C), F32),
            pltpu.VMEM((8, C), F32),
            pltpu.VMEM((8, C), F32),
            pltpu.VMEM((C, C), BF16),
            pltpu.VMEM((1, CELLS, C), BF16),
            pltpu.SemaphoreType.DMA((2, 3)),
        ],
        compiler_params=params,
        cost_estimate=pl.CostEstimate(
            flops=18 * 2 * CELLS * 9 * C * C, bytes_accessed=24 * 2**20, transcendentals=0
        ),
        name="rest",
    )(place, pieces, *shifted, recv, acc0, acc1, norm_gain, norm_bias, weight)
    back = lax.all_to_all(out, "space", 0, 0, tiled=True)
    shape = frames.shape
    return back[:, 0].reshape(shape), back[:, 1].reshape(shape)


def solution(mesh):
    in_specs = (
        P("stretch", "space", None, None),
        P("stretch", None),
        P(),
        P(),
        P(),
        P("stretch", "space", None, None),
    )
    out_specs = (P("stretch", "space", None, None), P("stretch", "space", None, None))
    return jax.shard_map(
        per_device, mesh=mesh, in_specs=in_specs, out_specs=out_specs, check_vma=False
    )
```

```python
import jax
import jax.numpy as jnp
from jax import lax
from jax.experimental import pallas as pl
from jax.experimental.pallas import tpu as pltpu
from jax.sharding import PartitionSpec as P

C = 384
GROUPS = 32
GSIZE = C // GROUPS
COLS = 32
ROWS = 8
CELLS = ROWS * COLS
PADDED = CELLS + 2 * COLS
COUNT = float(CELLS * GSIZE)
F32 = jnp.float32
BF16 = jnp.bfloat16
VMEM = pl.BlockSpec(memory_space=pltpu.VMEM)
SMEM = pl.BlockSpec(memory_space=pltpu.SMEM)
HBM = pl.BlockSpec(memory_space=pltpu.HBM)
ANY = pl.BlockSpec(memory_space=pl.ANY)


def group_matrix():
    row = lax.broadcasted_iota(jnp.int32, (C, C), 0) // GSIZE
    col = lax.broadcasted_iota(jnp.int32, (C, C), 1) // GSIZE
    return (row == col).astype(BF16)


def group_mean(sums, ones):
    n = sums.shape[0]
    high = sums.astype(BF16)
    rest = sums - high.astype(F32)
    mid = rest.astype(BF16)
    low = (rest - mid.astype(F32)).astype(BF16)
    parts = jnp.dot(
        jnp.concatenate([high.astype(F32), mid.astype(F32), low.astype(F32)], axis=0).astype(BF16),
        ones[...],
        preferred_element_type=F32,
    )
    return (parts[:n] + parts[n : 2 * n] + parts[2 * n :]) * (1.0 / COUNT)


def fold(values):
    return jnp.sum(values.reshape(COLS // 8, 8, C), axis=0)


def sigmoid(v):
    return 0.5 * jnp.tanh(0.5 * v) + 0.5


def store_shifted(slab, idx, row, values):
    col = lax.broadcasted_iota(jnp.int32, (COLS, C), 0)
    left = jnp.where(col == 0, 0.0, pltpu.roll(values, 1, 0))
    right = jnp.where(col == COLS - 1, 0.0, pltpu.roll(values, COLS - 1, 0))
    at = pl.ds(row * COLS, COLS)
    slab[idx, at, 0:C] = left.astype(BF16)
    slab[idx, at, C : 2 * C] = values.astype(BF16)
    slab[idx, at, 2 * C : 3 * C] = right.astype(BF16)


def conv_tap(slab_in, taps, a, acc, f):
    w = jnp.concatenate(
        [taps[pl.ds(a * 9 + 3 * b, 3)].reshape(3 * C, C) for b in range(3)], axis=1
    )
    y = jnp.dot(slab_in, w, preferred_element_type=F32)
    for b in range(3):
        acc[f, (2 - b) * COLS : (2 - b) * COLS + CELLS, :] += y[:, b * C : (b + 1) * C]


def adjoint_tap(slab_in, taps, a, acc, f):
    w = jnp.concatenate(
        [
            jnp.concatenate([taps[a * 9 + 3 * b + 2 - e] for e in range(3)], axis=1)
            for b in range(3)
        ],
        axis=0,
    )
    y = lax.dot_general(slab_in, w, (((1,), (1,)), ((), ())), preferred_element_type=F32)
    for b in range(3):
        acc[f, b * COLS : b * COLS + CELLS, :] += y[:, b * C : (b + 1) * C]


def frame_sums(x, idx):
    def body(r, tot):
        return tot + fold(x[idx, pl.ds(r * COLS, COLS), :].astype(F32))

    tot = lax.fori_loop(0, ROWS, body, jnp.zeros((8, C), F32), unroll=True)
    return jnp.sum(tot, axis=0, keepdims=True)


def frame_square_sums(x, idx, mean):
    def body(r, tot):
        diff = x[idx, pl.ds(r * COLS, COLS), :].astype(F32) - mean
        return tot + fold(diff * diff)

    tot = lax.fori_loop(0, ROWS, body, jnp.zeros((8, C), F32), unroll=True)
    return jnp.sum(tot, axis=0, keepdims=True)


def frame_stats(x, count, sums, mean, inv_std, ones):
    sums[...] = jnp.zeros_like(sums)

    def total(n, _):
        sums[pl.ds(n, 1), :] = frame_sums(x, n)
        return 0

    lax.fori_loop(0, count, total, 0)
    mean[...] = group_mean(sums[...], ones)

    def square(n, _):
        sums[pl.ds(n, 1), :] = frame_square_sums(x, n, mean[pl.ds(n, 1), :])
        return 0

    lax.fori_loop(0, count, square, 0)
    inv_std[...] = lax.rsqrt(group_mean(sums[...], ones) + 1e-5)


def norm_silu_frame(x, idx, mean, inv_std, gain, bias, slab, out_idx, mask):
    scale = inv_std * gain

    def body(r, _):
        v = (x[idx, pl.ds(r * COLS, COLS), :].astype(F32) - mean) * scale + bias
        s = v * sigmoid(v)
        if mask is not None:
            s = s * mask
        store_shifted(slab, out_idx, r, s)
        return 0

    lax.fori_loop(0, ROWS, body, 0, unroll=2)


def norm_back_sums(x, idx, mean, inv_std, gain, bias, acc, f):
    def body(r, tot):
        at = pl.ds(COLS + r * COLS, COLS)
        n = (x[idx, pl.ds(r * COLS, COLS), :].astype(F32) - mean) * inv_std
        v = n * gain + bias
        sig = sigmoid(v)
        gn = acc[f, at, :] * (sig * (1.0 + v * (1.0 - sig)) * gain)
        acc[f, at, :] = gn
        return tot[0] + fold(gn), tot[1] + fold(gn * n)

    zero = jnp.zeros((8, C), F32)
    one, two = lax.fori_loop(0, ROWS, body, (zero, zero), unroll=2)
    return jnp.sum(one, axis=0, keepdims=True), jnp.sum(two, axis=0, keepdims=True)


def norm_back_row(x, idx, r, mean, inv_std, acc, f, first, second):
    n = (x[idx, pl.ds(r * COLS, COLS), :].astype(F32) - mean) * inv_std
    return inv_std * (acc[f, pl.ds(COLS + r * COLS, COLS), :] - first - n * second)


def read_row(block):
    return jnp.concatenate([block(half) for half in range(2)], axis=0)


def layer_weights(weight, taps, sems, layer):
    return [
        pltpu.make_async_copy(
            weight.at[layer, pl.ds(a * 9, 9)], taps.at[layer, pl.ds(a * 9, 9)], sems.at[layer, a]
        )
        for a in range(3)
    ]


def start_weights(weight, taps, sems, layer):
    for copy in layer_weights(weight, taps, sems, layer):
        copy.start()


def wait_weights(weight, taps, sems, layer):
    for copy in layer_weights(weight, taps, sems, layer):
        copy.wait()
    if layer == 0:
        start_weights(weight, taps, sems, 1)


def prepare_kernel(table, frames, cot, pieces, *windows):
    for n, part in enumerate((frames, cot)):
        pieces[n * 16 : n * 16 + 16, 0:16, :] = part[...]
    row = lax.broadcasted_iota(jnp.int32, (8, C), 0)
    here = lax.broadcasted_iota(jnp.int32, (8, C), 1) == lax.axis_index("stretch")
    links = jnp.where(row == 0, table[0, 3], jnp.where(row == 1, table[0, 2], 0))
    links = jnp.where(here, links, 0).astype(F32).astype(BF16)
    for k in range(32):
        pieces[k, 16:24, :] = links
    for shift, window in enumerate(windows):
        first = (lax.rem(lax.axis_index("space") + shift + 1, 4) == 0).astype(jnp.int32)
        order = [(frames, g) for g in (3, 0, 1, 2)] + [(cot, g) for g in (3, 2, 1, 0)]
        for n, (part, g) in enumerate(order):

            @pl.when((n >= first) & (n < first + 7))
            def _(n=n, part=part, g=g, first=first, window=window):
                window[pl.ds((n - first) * 4, 4)] = part[g * 4 : g * 4 + 4]


def raw_block(j, g):
    first = (j == 0).astype(jnp.int32)
    return jnp.maximum(lax.rem(g + 1, 4) - first, 0) * 4


def cot_block(j, g):
    first = (j == 0).astype(jnp.int32)
    return jnp.minimum(7 - g - first, 6) * 4


def route_kernel(pieces, out, held, found, links, sem):
    block = lax.axis_index("stretch")
    g = lax.rem(block, 16) // 4
    raw = block < 16

    found[...] = sum(pieces[k, 16:24, 0:128].astype(F32) for k in range(32)).astype(jnp.int32)
    copy = pltpu.make_async_copy(found, links, sem)
    copy.start()
    held[0:32] = pieces[:, 0:16, :]
    held[32] = jnp.zeros((16, C), BF16)
    copy.wait()

    def body(d, _):
        prv, nxt = links[0, d], links[1, d]
        for j in range(4):
            raw_src = jnp.where(j <= g, prv, jnp.where(j >= g + 2, nxt, -1))
            src = jnp.where(raw, raw_src, jnp.where(j >= g, nxt, -1))
            out[d * 4 + j] = held[jnp.where(src < 0, 32, src)]
        return 0

    lax.fori_loop(0, 32, body, 0, unroll=4)


def own_kernel(
    table, mine, mine_cot, from1, from2, from3, gain, bias, weight, acc_out,
    taps, x, slab, gslab, acc, sums, mean, inv_std, ones, sems, save_sems,
):
    start_weights(weight, taps, sems, 0)
    j = lax.axis_index("space")
    ones[...] = group_matrix()
    acc[...] = jnp.zeros_like(acc)
    for shift, part in enumerate((None, from1, from2, from3)):
        holder = lax.rem(j + 4 - shift, 4)

        def rows(t, _, part=part, holder=holder):
            g, r = t // 2, lax.rem(t, 2)
            at = pl.ds((holder * 2 + r) * COLS, COLS)
            if part is None:
                x[g, at, :] = read_row(lambda half: mine[t * 2 + half])
                cot = read_row(lambda half: mine_cot[t * 2 + half])
            else:
                x[g, at, :] = read_row(lambda half: part[raw_block(j, g) + r * 2 + half])
                cot = read_row(lambda half: part[cot_block(j, g) + r * 2 + half])
            store_shifted(gslab, g, holder * 2 + r, cot.astype(F32))
            return 0

        lax.fori_loop(0, 8, rows, 0)
    frame_stats(x, 4, sums, mean, inv_std, ones)

    def normed(g, _):
        norm_silu_frame(
            x, g, mean[pl.ds(g, 1), :], inv_std[pl.ds(g, 1), :],
            gain[0:1, :], bias[0:1, :], slab, g, None,
        )
        return 0

    lax.fori_loop(0, 4, normed, 0)
    wait_weights(weight, taps, sems, 0)

    def forward(t, _):
        g, a = t // 3, lax.rem(t, 3)
        f = g + 4 - j - a

        @pl.when((f >= 0) & (f <= 4))
        def _():
            conv_tap(slab[g], taps.at[0], a, acc, f)

        return 0

    lax.fori_loop(0, 12, forward, 0)
    acc[8, 0:8] = mean[...]
    acc[8, 8:16] = inv_std[...]
    acc[8, COLS : COLS + CELLS] = x[j].astype(F32)
    saves = [
        pltpu.make_async_copy(acc.at[0:5], acc_out.at[0:5], save_sems.at[0]),
        pltpu.make_async_copy(acc.at[5:9], acc_out.at[5:9], save_sems.at[1]),
    ]
    saves[0].start()
    wait_weights(weight, taps, sems, 1)

    def backward(t, _):
        g, a = t // 3, lax.rem(t, 3)
        u = g - j
        f = u - 2 + a

        @pl.when((u >= 0) & (f >= 0) & (f <= 2))
        def _():
            adjoint_tap(gslab[g], taps.at[1], a, acc, 5 + f)

        return 0

    lax.fori_loop(0, 12, backward, 0)
    saves[1].start()
    for save in saves:
        save.wait()


def rest_kernel(
    table, recv, acc_in, gain, bias, weight, out,
    taps, x, slab, gslab, acc, acc2, h, sums, mean, inv_std, ones, sems, load_sem,
):
    load = pltpu.make_async_copy(acc_in.at[0:9], acc, load_sem)
    load.start()
    start_weights(weight, taps, sems, 0)
    j = lax.axis_index("space")
    has_prev = (table[0, 3] >= 0).astype(F32)
    ones[...] = group_matrix()

    def rows(t, _):
        g, row = t // 8, lax.rem(t, 8)
        i, r = row // 2, lax.rem(row, 2)
        x[g, pl.ds(row * COLS, COLS), :] = read_row(lambda half: recv[((g * 2 + r) * 2 + half) * 4 + i])
        cot = read_row(lambda half: recv[(16 + (g * 2 + r) * 2 + half) * 4 + i])
        store_shifted(gslab, g, row, cot.astype(F32))
        return 0

    lax.fori_loop(0, 32, rows, 0)
    frame_stats(x, 4, sums, mean, inv_std, ones)

    def normed(g, _):
        mask = jnp.where(g >= j, has_prev, 1.0)
        norm_silu_frame(
            x, g, mean[pl.ds(g, 1), :], inv_std[pl.ds(g, 1), :],
            gain[0:1, :], bias[0:1, :], slab, g, mask,
        )
        return 0

    lax.fori_loop(0, 4, normed, 0)
    load.wait()
    wait_weights(weight, taps, sems, 0)

    def forward(t, _):
        g, a = t // 3, lax.rem(t, 3)
        w = jnp.where(g >= j, g - j, g - j + 8)
        f = w - a

        @pl.when((f >= 0) & (f <= 4) & (g != j - 1))
        def _():
            conv_tap(slab[g], taps.at[0], a, acc, f)

        return 0

    lax.fori_loop(0, 12, forward, 0)
    wait_weights(weight, taps, sems, 1)

    def backward(t, _):
        g, a = t // 3, lax.rem(t, 3)
        u = g + 4 - j
        f = u - 2 + a

        @pl.when((u <= 4) & (f >= 0) & (f <= 2))
        def _():
            adjoint_tap(gslab[g], taps.at[1], a, acc, 5 + f)

        return 0

    lax.fori_loop(0, 12, backward, 0)

    def rounded(f, _):
        h[f] = acc[f, COLS : COLS + CELLS, :].astype(BF16)
        return 0

    lax.fori_loop(0, 5, rounded, 0)
    frame_stats(h, 5, sums, mean, inv_std, ones)
    gain1, bias1 = gain[1:2, :], bias[1:2, :]

    def normed1(f, _):
        mask = jnp.where(j - 2 + f < 0, has_prev, 1.0)
        norm_silu_frame(
            h, f, mean[pl.ds(f, 1), :], inv_std[pl.ds(f, 1), :], gain1, bias1, slab, f, mask
        )
        return 0

    lax.fori_loop(0, 3, normed1, 0)
    acc2[...] = jnp.zeros_like(acc2)

    def last(a, _):
        conv_tap(slab[a], taps.at[1], a, acc2, 0)
        return 0

    lax.fori_loop(0, 3, last, 0)
    for i in range(4):
        out[i, 0] = acc2[0, COLS + i * 64 : COLS + i * 64 + 64, :].astype(BF16)

    sums[...] = jnp.zeros_like(sums)

    def back_sums(f, _):
        n = f + 2
        one, two = norm_back_sums(
            h, n, mean[pl.ds(n, 1), :], inv_std[pl.ds(n, 1), :], gain1, bias1, acc, 5 + f
        )
        sums[pl.ds(f, 1), :] = one
        sums[pl.ds(f + 4, 1), :] = two
        return 0

    lax.fori_loop(0, 3, back_sums, 0)
    sums[...] = group_mean(sums[...], ones)

    def back_rows(t, _):
        f, r = t // 8, lax.rem(t, 8)
        n = f + 2
        g1 = norm_back_row(
            h, n, r, mean[pl.ds(n, 1), :], inv_std[pl.ds(n, 1), :], acc, 5 + f,
            sums[pl.ds(f, 1), :], sums[pl.ds(f + 4, 1), :],
        )
        store_shifted(slab, f, r, g1)
        return 0

    lax.fori_loop(0, 24, back_rows, 0)
    acc2[...] = jnp.zeros_like(acc2)

    def first(a, _):
        adjoint_tap(slab[2 - a], taps.at[0], a, acc2, 0)
        return 0

    lax.fori_loop(0, 3, first, 0)

    m0, i0 = acc[8, pl.ds(j, 1), :], acc[8, pl.ds(8 + j, 1), :]
    raw_own = acc.at[8:9, COLS : COLS + CELLS]
    one, two = norm_back_sums(raw_own, 0, m0, i0, gain[0:1, :], bias[0:1, :], acc2, 0)
    sums[0:1, :] = one
    sums[1:2, :] = two
    sums[...] = group_mean(sums[...], ones)
    for r in range(8):
        g0 = norm_back_row(raw_own, 0, r, m0, i0, acc2, 0, sums[0:1, :], sums[1:2, :])
        out[r // 2, 1, (r % 2) * COLS : (r % 2 + 1) * COLS, :] = g0.astype(BF16)


def per_device(frames, stretch_table, conv_weight, norm_gain, norm_bias, cotangent):
    params = pltpu.CompilerParams(vmem_limit_bytes=115 * 2**19)
    weight = conv_weight.reshape(2, 27, C, C)
    mine, mine_cot = frames.reshape(16, 16, C), cotangent.reshape(16, 16, C)
    pieces, *windows = pl.pallas_call(
        prepare_kernel,
        out_shape=[jax.ShapeDtypeStruct((32, 24, C), BF16)]
        + [jax.ShapeDtypeStruct((28, 16, C), BF16)] * 3,
        in_specs=[SMEM, VMEM, VMEM],
        out_specs=[VMEM] * 4,
        name="prepare",
    )(stretch_table, mine, mine_cot)
    shifted = [
        lax.ppermute(window, "space", [(i, (i + k) % 4) for i in range(4)])
        for k, window in zip((1, 2, 3), windows)
    ]
    spread = lax.cond(
        stretch_table[0, 0] >= -1,
        lambda p: lax.all_to_all(p, "stretch", 0, 0, tiled=True),
        lambda p: p,
        pieces,
    )
    spread, *shifted = lax.optimization_barrier((spread, *shifted))
    routed = pl.pallas_call(
        route_kernel,
        out_shape=jax.ShapeDtypeStruct((128, 16, C), BF16),
        in_specs=[VMEM],
        out_specs=VMEM,
        scratch_shapes=[
            pltpu.VMEM((33, 16, C), BF16),
            pltpu.VMEM((8, 128), jnp.int32),
            pltpu.SMEM((8, 128), jnp.int32),
            pltpu.SemaphoreType.DMA,
        ],
        name="route",
    )(spread)
    recv = lax.all_to_all(routed, ("stretch", "space"), 0, 0, tiled=True)
    acc = pl.pallas_call(
        own_kernel,
        out_shape=jax.ShapeDtypeStruct((32, PADDED, C), F32),
        in_specs=[SMEM] + [VMEM] * 7 + [ANY],
        out_specs=HBM,
        scratch_shapes=[
            pltpu.VMEM((2, 27, C, C), BF16),
            pltpu.VMEM((4, CELLS, C), BF16),
            pltpu.VMEM((4, CELLS, 3 * C), BF16),
            pltpu.VMEM((4, CELLS, 3 * C), BF16),
            pltpu.VMEM((9, PADDED, C), F32),
            pltpu.VMEM((8, C), F32),
            pltpu.VMEM((8, C), F32),
            pltpu.VMEM((8, C), F32),
            pltpu.VMEM((C, C), BF16),
            pltpu.SemaphoreType.DMA((2, 3)),
            pltpu.SemaphoreType.DMA((2,)),
        ],
        compiler_params=params,
        cost_estimate=pl.CostEstimate(
            flops=15 * 2 * CELLS * 9 * C * C, bytes_accessed=24 * 2**20, transcendentals=0
        ),
        name="own",
    )(stretch_table, mine, mine_cot, *shifted, norm_gain, norm_bias, weight)
    out = pl.pallas_call(
        rest_kernel,
        out_shape=jax.ShapeDtypeStruct((4, 2, 64, C), BF16),
        in_specs=[SMEM, VMEM, HBM, VMEM, VMEM, ANY],
        out_specs=VMEM,
        scratch_shapes=[
            pltpu.VMEM((2, 27, C, C), BF16),
            pltpu.VMEM((4, CELLS, C), BF16),
            pltpu.VMEM((4, CELLS, 3 * C), BF16),
            pltpu.VMEM((4, CELLS, 3 * C), BF16),
            pltpu.VMEM((9, PADDED, C), F32),
            pltpu.VMEM((1, PADDED, C), F32),
            pltpu.VMEM((5, CELLS, C), BF16),
            pltpu.VMEM((8, C), F32),
            pltpu.VMEM((8, C), F32),
            pltpu.VMEM((8, C), F32),
            pltpu.VMEM((C, C), BF16),
            pltpu.SemaphoreType.DMA((2, 3)),
            pltpu.SemaphoreType.DMA,
        ],
        compiler_params=pltpu.CompilerParams(vmem_limit_bytes=48 * 2**20),
        cost_estimate=pl.CostEstimate(
            flops=18 * 2 * CELLS * 9 * C * C, bytes_accessed=24 * 2**20, transcendentals=0
        ),
        name="rest",
    )(stretch_table, recv, acc, norm_gain, norm_bias, weight)
    back = lax.all_to_all(out, "space", 0, 0, tiled=True)
    shape = frames.shape
    return back[:, 0].reshape(shape), back[:, 1].reshape(shape)


def solution(mesh):
    in_specs = (
        P("stretch", "space", None, None),
        P("stretch", None),
        P(),
        P(),
        P(),
        P("stretch", "space", None, None),
    )
    out_specs = (P("stretch", "space", None, None), P("stretch", "space", None, None))
    return jax.shard_map(
        per_device, mesh=mesh, in_specs=in_specs, out_specs=out_specs, check_vma=False
    )
```

```python
import jax
import jax.numpy as jnp
from jax import lax
from jax.experimental import pallas as pl
from jax.experimental.pallas import tpu as pltpu
from jax.sharding import PartitionSpec as P

C = 384
GROUPS = 32
GSIZE = C // GROUPS
COLS = 32
ROWS = 8
CELLS = ROWS * COLS
PADDED = CELLS + 2 * COLS
COUNT = float(CELLS * GSIZE)
F32 = jnp.float32
BF16 = jnp.bfloat16
VMEM = pl.BlockSpec(memory_space=pltpu.VMEM)
SMEM = pl.BlockSpec(memory_space=pltpu.SMEM)
HBM = pl.BlockSpec(memory_space=pltpu.HBM)
ANY = pl.BlockSpec(memory_space=pl.ANY)


def group_matrix():
    row = lax.broadcasted_iota(jnp.int32, (C, C), 0) // GSIZE
    col = lax.broadcasted_iota(jnp.int32, (C, C), 1) // GSIZE
    return (row == col).astype(BF16)


def group_mean(sums, ones):
    n = sums.shape[0]
    high = sums.astype(BF16)
    rest = sums - high.astype(F32)
    mid = rest.astype(BF16)
    low = (rest - mid.astype(F32)).astype(BF16)
    parts = jnp.dot(
        jnp.concatenate([high.astype(F32), mid.astype(F32), low.astype(F32)], axis=0).astype(BF16),
        ones[...],
        preferred_element_type=F32,
    )
    return (parts[:n] + parts[n : 2 * n] + parts[2 * n :]) * (1.0 / COUNT)


def fold(values):
    return jnp.sum(values.reshape(COLS // 8, 8, C), axis=0)


def sigmoid(v):
    return 0.5 * jnp.tanh(0.5 * v) + 0.5


def store_shifted(slab, idx, row, values):
    col = lax.broadcasted_iota(jnp.int32, (COLS, C), 0)
    left = jnp.where(col == 0, 0.0, pltpu.roll(values, 1, 0))
    right = jnp.where(col == COLS - 1, 0.0, pltpu.roll(values, COLS - 1, 0))
    at = pl.ds(row * COLS, COLS)
    slab[idx, at, 0:C] = left.astype(BF16)
    slab[idx, at, C : 2 * C] = values.astype(BF16)
    slab[idx, at, 2 * C : 3 * C] = right.astype(BF16)


def conv_taps(slab, first, taps, a, n, acc, f):
    cells = jnp.concatenate([slab[first + i] for i in range(n)], axis=1)
    w = jnp.concatenate(
        [
            jnp.concatenate(
                [taps[pl.ds((a + i) * 9 + 3 * b, 3)].reshape(3 * C, C) for b in range(3)], axis=1
            )
            for i in range(n)
        ],
        axis=0,
    )
    y = jnp.dot(cells, w, preferred_element_type=F32)
    for b in range(3):
        acc[f, (2 - b) * COLS : (2 - b) * COLS + CELLS, :] += y[:, b * C : (b + 1) * C]


def adjoint_taps(slab, first, taps, a, n, acc, f):
    cells = jnp.concatenate([slab[first - i] for i in range(n)], axis=1)
    w = jnp.concatenate(
        [
            jnp.concatenate(
                [taps[(a + i) * 9 + 3 * b + 2 - e] for i in range(n) for e in range(3)], axis=1
            )
            for b in range(3)
        ],
        axis=0,
    )
    y = lax.dot_general(cells, w, (((1,), (1,)), ((), ())), preferred_element_type=F32)
    for b in range(3):
        acc[f, b * COLS : b * COLS + CELLS, :] += y[:, b * C : (b + 1) * C]


def by_count(step, slab, first, taps, a, n, acc, f):
    for count in (1, 2, 3):

        @pl.when(n == count)
        def _(count=count):
            step(slab, first, taps, a, count, acc, f)


def frame_sums(x, idx):
    def body(r, tot):
        return tot + fold(x[idx, pl.ds(r * COLS, COLS), :].astype(F32))

    tot = lax.fori_loop(0, ROWS, body, jnp.zeros((8, C), F32), unroll=True)
    return jnp.sum(tot, axis=0, keepdims=True)


def frame_square_sums(x, idx, mean):
    def body(r, tot):
        diff = x[idx, pl.ds(r * COLS, COLS), :].astype(F32) - mean
        return tot + fold(diff * diff)

    tot = lax.fori_loop(0, ROWS, body, jnp.zeros((8, C), F32), unroll=True)
    return jnp.sum(tot, axis=0, keepdims=True)


def frame_stats(x, count, sums, mean, inv_std, ones):
    sums[...] = jnp.zeros_like(sums)

    def total(n, _):
        sums[pl.ds(n, 1), :] = frame_sums(x, n)
        return 0

    lax.fori_loop(0, count, total, 0)
    mean[...] = group_mean(sums[...], ones)

    def square(n, _):
        sums[pl.ds(n, 1), :] = frame_square_sums(x, n, mean[pl.ds(n, 1), :])
        return 0

    lax.fori_loop(0, count, square, 0)
    inv_std[...] = lax.rsqrt(group_mean(sums[...], ones) + 1e-5)


def norm_silu_frame(x, idx, mean, inv_std, gain, bias, slab, out_idx, mask):
    scale = inv_std * gain

    def body(r, _):
        v = (x[idx, pl.ds(r * COLS, COLS), :].astype(F32) - mean) * scale + bias
        s = v * sigmoid(v)
        if mask is not None:
            s = s * mask
        store_shifted(slab, out_idx, r, s)
        return 0

    lax.fori_loop(0, ROWS, body, 0, unroll=2)


def norm_back_sums(x, idx, mean, inv_std, gain, bias, acc, f):
    def body(r, tot):
        at = pl.ds(COLS + r * COLS, COLS)
        n = (x[idx, pl.ds(r * COLS, COLS), :].astype(F32) - mean) * inv_std
        v = n * gain + bias
        sig = sigmoid(v)
        gn = acc[f, at, :] * (sig * (1.0 + v * (1.0 - sig)) * gain)
        acc[f, at, :] = gn
        return tot[0] + fold(gn), tot[1] + fold(gn * n)

    zero = jnp.zeros((8, C), F32)
    one, two = lax.fori_loop(0, ROWS, body, (zero, zero), unroll=2)
    return jnp.sum(one, axis=0, keepdims=True), jnp.sum(two, axis=0, keepdims=True)


def norm_back_row(x, idx, r, mean, inv_std, acc, f, first, second):
    n = (x[idx, pl.ds(r * COLS, COLS), :].astype(F32) - mean) * inv_std
    return inv_std * (acc[f, pl.ds(COLS + r * COLS, COLS), :] - first - n * second)


def read_row(block):
    return jnp.concatenate([block(half) for half in range(2)], axis=0)


def layer_weights(weight, taps, sems, layer):
    return [
        pltpu.make_async_copy(
            weight.at[layer, pl.ds(a * 9, 9)], taps.at[layer, pl.ds(a * 9, 9)], sems.at[layer, a]
        )
        for a in range(3)
    ]


def start_weights(weight, taps, sems, layer):
    for copy in layer_weights(weight, taps, sems, layer):
        copy.start()


def wait_weights(weight, taps, sems, layer):
    for copy in layer_weights(weight, taps, sems, layer):
        copy.wait()
    if layer == 0:
        start_weights(weight, taps, sems, 1)


def prepare_kernel(table, frames, cot, pieces, *windows):
    for n, part in enumerate((frames, cot)):
        for c in range(3):
            pieces[n * 16 : n * 16 + 16, c * 16 : c * 16 + 16, :] = part[:, :, c * 128 : c * 128 + 128]
    row = lax.broadcasted_iota(jnp.int32, (8, 128), 0)
    here = lax.broadcasted_iota(jnp.int32, (8, 128), 1) == lax.axis_index("stretch")
    links = jnp.where(row == 0, table[0, 3], jnp.where(row == 1, table[0, 2], 0))
    links = jnp.where(here, links, 0).astype(F32).astype(BF16)
    for k in range(32):
        pieces[k, 48:56, :] = links
    for shift, window in enumerate(windows):
        first = (lax.rem(lax.axis_index("space") + shift + 1, 4) == 0).astype(jnp.int32)
        order = [(frames, g) for g in (3, 0, 1, 2)] + [(cot, g) for g in (3, 2, 1, 0)]
        for n, (part, g) in enumerate(order):

            @pl.when((n >= first) & (n < first + 7))
            def _(n=n, part=part, g=g, first=first, window=window):
                window[pl.ds((n - first) * 4, 4)] = part[g * 4 : g * 4 + 4]


def raw_block(j, g):
    first = (j == 0).astype(jnp.int32)
    return jnp.maximum(lax.rem(g + 1, 4) - first, 0) * 4


def cot_block(j, g):
    first = (j == 0).astype(jnp.int32)
    return jnp.minimum(7 - g - first, 6) * 4


def route_kernel(pieces, out, held, found, links, sem):
    block = lax.axis_index("stretch")
    g = lax.rem(block, 16) // 4
    raw = block < 16

    found[...] = sum(pieces[k, 48:56, :].astype(F32) for k in range(32)).astype(jnp.int32)
    copy = pltpu.make_async_copy(found, links, sem)
    copy.start()
    for c in range(3):
        held[0:32, :, c * 128 : c * 128 + 128] = pieces[:, c * 16 : c * 16 + 16, :]
    held[32] = jnp.zeros((16, C), BF16)
    copy.wait()

    def body(d, _):
        prv, nxt = links[0, d], links[1, d]
        for j in range(4):
            raw_src = jnp.where(j <= g, prv, jnp.where(j >= g + 2, nxt, -1))
            src = jnp.where(raw, raw_src, jnp.where(j >= g, nxt, -1))
            out[d * 4 + j] = held[jnp.where(src < 0, 32, src)]
        return 0

    lax.fori_loop(0, 32, body, 0, unroll=4)


def own_kernel(
    table, mine, mine_cot, from1, from2, from3, gain, bias, weight, acc_out,
    taps, x, slab, gslab, acc, h, sums, mean, inv_std, ones, sems, save_sems,
):
    start_weights(weight, taps, sems, 0)
    j = lax.axis_index("space")
    ones[...] = group_matrix()
    acc[...] = jnp.zeros_like(acc)
    for shift, part in enumerate((None, from1, from2, from3)):
        holder = lax.rem(j + 4 - shift, 4)

        def rows(t, _, part=part, holder=holder):
            g, r = t // 2, lax.rem(t, 2)
            at = pl.ds((holder * 2 + r) * COLS, COLS)
            if part is None:
                x[g, at, :] = read_row(lambda half: mine[t * 2 + half])
                cot = read_row(lambda half: mine_cot[t * 2 + half])
            else:
                x[g, at, :] = read_row(lambda half: part[raw_block(j, g) + r * 2 + half])
                cot = read_row(lambda half: part[cot_block(j, g) + r * 2 + half])
            store_shifted(gslab, g, holder * 2 + r, cot.astype(F32))
            return 0

        lax.fori_loop(0, 8, rows, 0)
    frame_stats(x, 4, sums, mean, inv_std, ones)

    def normed(g, _):
        norm_silu_frame(
            x, g, mean[pl.ds(g, 1), :], inv_std[pl.ds(g, 1), :],
            gain[0:1, :], bias[0:1, :], slab, g, None,
        )
        return 0

    lax.fori_loop(0, 4, normed, 0)
    wait_weights(weight, taps, sems, 0)

    def forward(f, _):
        low = jnp.maximum(0, 4 - j - f)
        n = jnp.minimum(2, 7 - j - f) - low + 1
        by_count(conv_taps, slab, f + low - 4 + j, taps.at[0], low, n, acc, f)
        return 0

    lax.fori_loop(0, 5, forward, 0)
    acc[8, 0:8] = mean[...]
    acc[8, 8:16] = inv_std[...]
    acc[8, COLS : COLS + CELLS] = x[j].astype(F32)
    saves = [
        pltpu.make_async_copy(acc.at[0:5], acc_out.at[0:5], save_sems.at[0]),
        pltpu.make_async_copy(acc.at[5:10], acc_out.at[5:10], save_sems.at[1]),
    ]
    saves[0].start()
    wait_weights(weight, taps, sems, 1)

    def backward(f, _):
        low = jnp.maximum(0, f + j - 1)
        by_count(adjoint_taps, gslab, j + f + 2 - low, taps.at[1], low, 3 - low, acc, 5 + f)
        return 0

    lax.fori_loop(0, 3, backward, 0)

    @pl.when(j >= 2)
    def _():
        for n in range(2):
            h[n] = acc[1 + n, COLS : COLS + CELLS, :].astype(BF16)
        frame_stats(h, 2, sums, mean, inv_std, ones)

        def normed1(n, _):
            norm_silu_frame(
                h, n, mean[pl.ds(n, 1), :], inv_std[pl.ds(n, 1), :],
                gain[1:2, :], bias[1:2, :], slab, n, None,
            )
            return 0

        lax.fori_loop(0, 2, normed1, 0)
        by_count(conv_taps, slab, 3 - j, taps.at[1], 4 - j, j - 1, acc, 9)

    saves[1].start()
    for save in saves:
        save.wait()


def rest_kernel(
    table, recv, acc_in, gain, bias, weight, out,
    taps, x, slab, gslab, acc, acc2, h, sums, mean, inv_std, ones, sems, load_sem,
):
    load = pltpu.make_async_copy(acc_in.at[0:10], acc, load_sem)
    load.start()
    start_weights(weight, taps, sems, 0)
    j = lax.axis_index("space")
    has_prev = (table[0, 3] >= 0).astype(F32)
    ones[...] = group_matrix()

    def rows(t, _):
        g, row = t // 8, lax.rem(t, 8)
        block = (g * 2 + lax.rem(row, 2)) * 2
        x[g, pl.ds(row * COLS, COLS), :] = read_row(lambda half: recv[(block + half) * 4 + row // 2])
        return 0

    def cot_rows(t, _):
        g, row = t // 8, lax.rem(t, 8)
        block = 16 + (g * 2 + lax.rem(row, 2)) * 2
        cot = read_row(lambda half: recv[(block + half) * 4 + row // 2])
        store_shifted(gslab, g, row, cot.astype(F32))
        return 0

    lax.fori_loop(0, 32, rows, 0)
    frame_stats(x, 4, sums, mean, inv_std, ones)

    def normed(g, _):
        mask = jnp.where(g >= j, has_prev, 1.0)
        norm_silu_frame(
            x, g, mean[pl.ds(g, 1), :], inv_std[pl.ds(g, 1), :],
            gain[0:1, :], bias[0:1, :], slab, g, mask,
        )
        return 0

    lax.fori_loop(0, 4, normed, 0)
    lax.fori_loop(0, 8 * (j + 1), cot_rows, 0)
    load.wait()
    wait_weights(weight, taps, sems, 0)

    def forward(f, _):
        prev = f < 4 - j
        low = jnp.where(prev, 0, jnp.maximum(0, 8 - j - f))
        n = jnp.where(prev, jnp.minimum(2, 3 - j - f), 2) - low + 1
        first = jnp.where(prev, j + f, f + low - 8 + j)
        by_count(conv_taps, slab, first, taps.at[0], low, n, acc, f)
        return 0

    lax.fori_loop(0, 5, forward, 0)
    wait_weights(weight, taps, sems, 1)

    def backward(f, _):
        n = jnp.minimum(2, f + j - 2) + 1
        by_count(adjoint_taps, gslab, f - 2 + j, taps.at[1], 0, n, acc, 5 + f)
        return 0

    lax.fori_loop(0, 3, backward, 0)

    def rounded(f, _):
        h[f] = acc[f, COLS : COLS + CELLS, :].astype(BF16)
        return 0

    lax.fori_loop(0, 5, rounded, 0)
    frame_stats(h, 5, sums, mean, inv_std, ones)
    gain1, bias1 = gain[1:2, :], bias[1:2, :]

    def normed1(f, _):
        mask = jnp.where(j - 2 + f < 0, has_prev, 1.0)
        norm_silu_frame(
            h, f, mean[pl.ds(f, 1), :], inv_std[pl.ds(f, 1), :], gain1, bias1, slab, f, mask
        )
        return 0

    lax.fori_loop(0, 3, normed1, 0)
    by_count(conv_taps, slab, 0, taps.at[1], 0, jnp.minimum(3, 4 - j), acc, 9)
    for i in range(4):
        out[i, 0] = acc[9, COLS + i * 64 : COLS + i * 64 + 64, :].astype(BF16)

    sums[...] = jnp.zeros_like(sums)

    def back_sums(f, _):
        n = f + 2
        one, two = norm_back_sums(
            h, n, mean[pl.ds(n, 1), :], inv_std[pl.ds(n, 1), :], gain1, bias1, acc, 5 + f
        )
        sums[pl.ds(f, 1), :] = one
        sums[pl.ds(f + 4, 1), :] = two
        return 0

    lax.fori_loop(0, 3, back_sums, 0)
    sums[...] = group_mean(sums[...], ones)

    def back_rows(t, _):
        f, r = t // 8, lax.rem(t, 8)
        n = f + 2
        g1 = norm_back_row(
            h, n, r, mean[pl.ds(n, 1), :], inv_std[pl.ds(n, 1), :], acc, 5 + f,
            sums[pl.ds(f, 1), :], sums[pl.ds(f + 4, 1), :],
        )
        store_shifted(slab, f, r, g1)
        return 0

    lax.fori_loop(0, 24, back_rows, 0)
    acc2[...] = jnp.zeros_like(acc2)

    adjoint_taps(slab, 2, taps.at[0], 0, 3, acc2, 0)

    m0, i0 = acc[8, pl.ds(j, 1), :], acc[8, pl.ds(8 + j, 1), :]
    raw_own = acc.at[8:9, COLS : COLS + CELLS]
    one, two = norm_back_sums(raw_own, 0, m0, i0, gain[0:1, :], bias[0:1, :], acc2, 0)
    sums[0:1, :] = one
    sums[1:2, :] = two
    sums[...] = group_mean(sums[...], ones)
    for r in range(8):
        g0 = norm_back_row(raw_own, 0, r, m0, i0, acc2, 0, sums[0:1, :], sums[1:2, :])
        out[r // 2, 1, (r % 2) * COLS : (r % 2 + 1) * COLS, :] = g0.astype(BF16)


def per_device(frames, stretch_table, conv_weight, norm_gain, norm_bias, cotangent):
    small = pltpu.CompilerParams(vmem_limit_bytes=8 * 2**20)
    params = pltpu.CompilerParams(vmem_limit_bytes=115 * 2**19)
    weight = conv_weight.reshape(2, 27, C, C)
    mine, mine_cot = frames.reshape(16, 16, C), cotangent.reshape(16, 16, C)
    pieces, *windows = pl.pallas_call(
        prepare_kernel,
        out_shape=[jax.ShapeDtypeStruct((32, 56, 128), BF16)]
        + [jax.ShapeDtypeStruct((28, 16, C), BF16)] * 3,
        in_specs=[SMEM, VMEM, VMEM],
        out_specs=[VMEM] * 4,
        name="prepare",
    )(stretch_table, mine, mine_cot)
    shifted = [
        lax.ppermute(window, "space", [(i, (i + k) % 4) for i in range(4)])
        for k, window in zip((1, 2, 3), windows)
    ]
    spread = lax.all_to_all(pieces, "stretch", 0, 0, tiled=True)
    routed = pl.pallas_call(
        route_kernel,
        out_shape=jax.ShapeDtypeStruct((128, 16, C), BF16),
        in_specs=[VMEM],
        out_specs=VMEM,
        scratch_shapes=[
            pltpu.VMEM((33, 16, C), BF16),
            pltpu.VMEM((8, 128), jnp.int32),
            pltpu.SMEM((8, 128), jnp.int32),
            pltpu.SemaphoreType.DMA,
        ],
        compiler_params=small,
        name="route",
    )(spread)
    recv = lax.all_to_all(routed, ("stretch", "space"), 0, 0, tiled=True)
    acc = pl.pallas_call(
        own_kernel,
        out_shape=jax.ShapeDtypeStruct((32, PADDED, C), F32),
        in_specs=[SMEM] + [VMEM] * 7 + [ANY],
        out_specs=HBM,
        scratch_shapes=[
            pltpu.VMEM((2, 27, C, C), BF16),
            pltpu.VMEM((4, CELLS, C), BF16),
            pltpu.VMEM((4, CELLS, 3 * C), BF16),
            pltpu.VMEM((4, CELLS, 3 * C), BF16),
            pltpu.VMEM((10, PADDED, C), F32),
            pltpu.VMEM((2, CELLS, C), BF16),
            pltpu.VMEM((8, C), F32),
            pltpu.VMEM((8, C), F32),
            pltpu.VMEM((8, C), F32),
            pltpu.VMEM((C, C), BF16),
            pltpu.SemaphoreType.DMA((2, 3)),
            pltpu.SemaphoreType.DMA((2,)),
        ],
        compiler_params=params,
        cost_estimate=pl.CostEstimate(
            flops=1500 * 2 * CELLS * 9 * C * C, bytes_accessed=24 * 2**20, transcendentals=0
        ),
        name="own",
    )(stretch_table, mine, mine_cot, *shifted, norm_gain, norm_bias, weight)
    out = pl.pallas_call(
        rest_kernel,
        out_shape=jax.ShapeDtypeStruct((4, 2, 64, C), BF16),
        in_specs=[SMEM, VMEM, HBM, VMEM, VMEM, ANY],
        out_specs=VMEM,
        scratch_shapes=[
            pltpu.VMEM((2, 27, C, C), BF16),
            pltpu.VMEM((4, CELLS, C), BF16),
            pltpu.VMEM((4, CELLS, 3 * C), BF16),
            pltpu.VMEM((4, CELLS, 3 * C), BF16),
            pltpu.VMEM((10, PADDED, C), F32),
            pltpu.VMEM((1, PADDED, C), F32),
            pltpu.VMEM((5, CELLS, C), BF16),
            pltpu.VMEM((8, C), F32),
            pltpu.VMEM((8, C), F32),
            pltpu.VMEM((8, C), F32),
            pltpu.VMEM((C, C), BF16),
            pltpu.SemaphoreType.DMA((2, 3)),
            pltpu.SemaphoreType.DMA,
        ],
        compiler_params=pltpu.CompilerParams(vmem_limit_bytes=48 * 2**20),
        cost_estimate=pl.CostEstimate(
            flops=18 * 2 * CELLS * 9 * C * C, bytes_accessed=24 * 2**20, transcendentals=0
        ),
        name="rest",
    )(stretch_table, recv, acc, norm_gain, norm_bias, weight)
    back = lax.all_to_all(out, "space", 0, 0, tiled=True)
    shape = frames.shape
    return back[:, 0].reshape(shape), back[:, 1].reshape(shape)


def solution(mesh):
    in_specs = (
        P("stretch", "space", None, None),
        P("stretch", None),
        P(),
        P(),
        P(),
        P("stretch", "space", None, None),
    )
    out_specs = (P("stretch", "space", None, None), P("stretch", "space", None, None))
    return jax.shard_map(
        per_device, mesh=mesh, in_specs=in_specs, out_specs=out_specs, check_vma=False
    )
```

```python
import jax
import jax.numpy as jnp
from jax import lax
from jax.experimental import pallas as pl
from jax.experimental.pallas import tpu as pltpu
from jax.sharding import PartitionSpec as P

C = 384
GROUPS = 32
GSIZE = C // GROUPS
COLS = 32
ROWS = 8
CELLS = ROWS * COLS
PADDED = CELLS + 2 * COLS
COUNT = float(CELLS * GSIZE)
F32 = jnp.float32
BF16 = jnp.bfloat16
VMEM = pl.BlockSpec(memory_space=pltpu.VMEM)
SMEM = pl.BlockSpec(memory_space=pltpu.SMEM)
HBM = pl.BlockSpec(memory_space=pltpu.HBM)
ANY = pl.BlockSpec(memory_space=pl.ANY)


def group_matrix():
    row = lax.broadcasted_iota(jnp.int32, (C, C), 0) // GSIZE
    col = lax.broadcasted_iota(jnp.int32, (C, C), 1) // GSIZE
    return (row == col).astype(BF16)


def group_mean(sums, ones):
    n = sums.shape[0]
    high = sums.astype(BF16)
    rest = sums - high.astype(F32)
    mid = rest.astype(BF16)
    low = (rest - mid.astype(F32)).astype(BF16)
    parts = jnp.dot(
        jnp.concatenate([high.astype(F32), mid.astype(F32), low.astype(F32)], axis=0).astype(BF16),
        ones[...],
        preferred_element_type=F32,
    )
    return (parts[:n] + parts[n : 2 * n] + parts[2 * n :]) * (1.0 / COUNT)


def fold(values):
    return jnp.sum(values.reshape(COLS // 8, 8, C), axis=0)


def sigmoid(v):
    return 0.5 * jnp.tanh(0.5 * v) + 0.5


def store_shifted(slab, idx, row, values):
    col = lax.broadcasted_iota(jnp.int32, (COLS, C), 0)
    left = jnp.where(col == 0, 0.0, pltpu.roll(values, 1, 0))
    right = jnp.where(col == COLS - 1, 0.0, pltpu.roll(values, COLS - 1, 0))
    at = pl.ds(row * COLS, COLS)
    slab[idx, at, 0:C] = left.astype(BF16)
    slab[idx, at, C : 2 * C] = values.astype(BF16)
    slab[idx, at, 2 * C : 3 * C] = right.astype(BF16)


def conv_taps(slab, first, taps, a, n, acc, f):
    cells = jnp.concatenate([slab[first + i] for i in range(n)], axis=1)
    w = jnp.concatenate(
        [
            jnp.concatenate(
                [taps[pl.ds((a + i) * 9 + 3 * b, 3)].reshape(3 * C, C) for b in range(3)], axis=1
            )
            for i in range(n)
        ],
        axis=0,
    )
    y = jnp.dot(cells, w, preferred_element_type=F32)
    for b in range(3):
        acc[f, (2 - b) * COLS : (2 - b) * COLS + CELLS, :] += y[:, b * C : (b + 1) * C]


def adjoint_taps(slab, first, taps, a, n, acc, f):
    cells = jnp.concatenate([slab[first - i] for i in range(n)], axis=1)
    w = jnp.concatenate(
        [
            jnp.concatenate(
                [taps[(a + i) * 9 + 3 * b + 2 - e] for i in range(n) for e in range(3)], axis=1
            )
            for b in range(3)
        ],
        axis=0,
    )
    y = lax.dot_general(cells, w, (((1,), (1,)), ((), ())), preferred_element_type=F32)
    for b in range(3):
        acc[f, b * COLS : b * COLS + CELLS, :] += y[:, b * C : (b + 1) * C]


def by_count(step, slab, first, taps, a, n, acc, f):
    for count in (1, 2, 3):

        @pl.when(n == count)
        def _(count=count):
            step(slab, first, taps, a, count, acc, f)


def frame_sums(x, idx):
    def body(r, tot):
        return tot + fold(x[idx, pl.ds(r * COLS, COLS), :].astype(F32))

    tot = lax.fori_loop(0, ROWS, body, jnp.zeros((8, C), F32), unroll=True)
    return jnp.sum(tot, axis=0, keepdims=True)


def frame_square_sums(x, idx, mean):
    def body(r, tot):
        diff = x[idx, pl.ds(r * COLS, COLS), :].astype(F32) - mean
        return tot + fold(diff * diff)

    tot = lax.fori_loop(0, ROWS, body, jnp.zeros((8, C), F32), unroll=True)
    return jnp.sum(tot, axis=0, keepdims=True)


def frame_stats(x, count, sums, mean, inv_std, ones):
    sums[...] = jnp.zeros_like(sums)

    def total(n, _):
        sums[pl.ds(n, 1), :] = frame_sums(x, n)
        return 0

    lax.fori_loop(0, count, total, 0)
    mean[...] = group_mean(sums[...], ones)

    def square(n, _):
        sums[pl.ds(n, 1), :] = frame_square_sums(x, n, mean[pl.ds(n, 1), :])
        return 0

    lax.fori_loop(0, count, square, 0)
    inv_std[...] = lax.rsqrt(group_mean(sums[...], ones) + 1e-5)


def norm_silu_frame(x, idx, mean, inv_std, gain, bias, slab, out_idx, mask):
    scale = inv_std * gain

    def body(r, _):
        v = (x[idx, pl.ds(r * COLS, COLS), :].astype(F32) - mean) * scale + bias
        s = v * sigmoid(v)
        if mask is not None:
            s = s * mask
        store_shifted(slab, out_idx, r, s)
        return 0

    lax.fori_loop(0, ROWS, body, 0, unroll=4)


def norm_back_sums(x, idx, mean, inv_std, gain, bias, acc, f, share):
    def body(r, tot):
        at = pl.ds(COLS + r * COLS, COLS)
        n = (x[idx, pl.ds(r * COLS, COLS), :].astype(F32) - mean) * inv_std
        v = n * gain + bias
        sig = sigmoid(v)
        upstream = acc[f, at, :] if share is None else acc[f, at, :] + share[f, at, :]
        gn = upstream * (sig * (1.0 + v * (1.0 - sig)) * gain)
        acc[f, at, :] = gn
        return tot[0] + fold(gn), tot[1] + fold(gn * n)

    zero = jnp.zeros((8, C), F32)
    one, two = lax.fori_loop(0, ROWS, body, (zero, zero), unroll=4)
    return jnp.sum(one, axis=0, keepdims=True), jnp.sum(two, axis=0, keepdims=True)


def norm_back_row(x, idx, r, mean, inv_std, acc, f, first, second):
    n = (x[idx, pl.ds(r * COLS, COLS), :].astype(F32) - mean) * inv_std
    return inv_std * (acc[f, pl.ds(COLS + r * COLS, COLS), :] - first - n * second)


def read_row(block):
    return jnp.concatenate([block(half) for half in range(2)], axis=0)


def layer_weights(weight, taps, sems, layer):
    return [
        pltpu.make_async_copy(
            weight.at[layer, pl.ds(a * 9, 9)], taps.at[layer, pl.ds(a * 9, 9)], sems.at[layer, a]
        )
        for a in range(3)
    ]


def start_weights(weight, taps, sems, layer):
    for copy in layer_weights(weight, taps, sems, layer):
        copy.start()


def wait_weights(weight, taps, sems, layer):
    for copy in layer_weights(weight, taps, sems, layer):
        copy.wait()


def prepare_kernel(table, frames, cot, pieces, *windows):
    for n, part in enumerate((frames, cot)):
        for c in range(3):
            pieces[n * 16 : n * 16 + 16, c * 16 : c * 16 + 16, :] = part[:, :, c * 128 : c * 128 + 128]
    row = lax.broadcasted_iota(jnp.int32, (8, 128), 0)
    here = lax.broadcasted_iota(jnp.int32, (8, 128), 1) == lax.axis_index("stretch")
    links = jnp.where(row == 0, table[0, 3], jnp.where(row == 1, table[0, 2], 0))
    links = jnp.where(here, links, 0).astype(F32).astype(BF16)
    for k in range(32):
        pieces[k, 48:56, :] = links
    for shift, window in enumerate(windows):
        first = (lax.rem(lax.axis_index("space") + shift + 1, 4) == 0).astype(jnp.int32)
        order = [(frames, g) for g in (3, 0, 1, 2)] + [(cot, g) for g in (3, 2, 1, 0)]
        for n, (part, g) in enumerate(order):

            @pl.when((n >= first) & (n < first + 7))
            def _(n=n, part=part, g=g, first=first, window=window):
                window[pl.ds((n - first) * 4, 4)] = part[g * 4 : g * 4 + 4]


def raw_block(j, g):
    first = (j == 0).astype(jnp.int32)
    return jnp.maximum(lax.rem(g + 1, 4) - first, 0) * 4


def cot_block(j, g):
    first = (j == 0).astype(jnp.int32)
    return jnp.minimum(7 - g - first, 6) * 4


def route_kernel(pieces, out, held, found, links, sorted_blocks, sem, out_sems):
    block = lax.axis_index("stretch")
    g = lax.rem(block, 16) // 4
    raw = block < 16

    found[...] = sum(pieces[k, 48:56, :].astype(F32) for k in range(32)).astype(jnp.int32)
    copy = pltpu.make_async_copy(found, links, sem)
    copy.start()
    for c in range(3):
        held[0:32, :, c * 128 : c * 128 + 128] = pieces[:, c * 16 : c * 16 + 16, :]
    held[32] = jnp.zeros((16, C), BF16)
    copy.wait()

    def body(d, _):
        prv, nxt = links[0, d], links[1, d]
        for j in range(4):
            raw_src = jnp.where(j <= g, prv, jnp.where(j >= g + 2, nxt, -1))
            src = jnp.where(raw, raw_src, jnp.where(j >= g, nxt, -1))
            sorted_blocks[d * 4 + j] = held[jnp.where(src < 0, 32, src)]
        return 0

    sends = []
    for part in range(4):
        lax.fori_loop(part * 8, part * 8 + 8, body, 0, unroll=4)
        at = pl.ds(part * 32, 32)
        sends.append(pltpu.make_async_copy(sorted_blocks.at[at], out.at[at], out_sems.at[part]))
        sends[-1].start()
    for send in sends:
        send.wait()


def share_copies(src, dst, sems):
    inner = pl.ds(COLS, CELLS)
    parts = [(pl.ds(0, 5), inner), (8,), (pl.ds(5, 3), inner), (9, inner)]
    return [
        pltpu.make_async_copy(src.at[part], dst.at[part], sems.at[n])
        for n, part in enumerate(parts)
    ]


def own_kernel(
    table, mine, mine_cot, from1, from2, from3, gain, bias, weight, acc_out,
    taps, x, slab, gslab, acc, h, sums, mean, inv_std, ones, sems, save_sems,
):
    start_weights(weight, taps, sems, 0)
    j = lax.axis_index("space")
    ones[...] = group_matrix()
    acc[...] = jnp.zeros_like(acc)
    for shift, part in enumerate((None, from1, from2, from3)):
        holder = lax.rem(j + 4 - shift, 4)

        def rows(t, _, part=part, holder=holder):
            g, r = t // 2, lax.rem(t, 2)
            at = pl.ds((holder * 2 + r) * COLS, COLS)
            if part is None:
                x[g, at, :] = read_row(lambda half: mine[t * 2 + half])
                cot = read_row(lambda half: mine_cot[t * 2 + half])
            else:
                x[g, at, :] = read_row(lambda half: part[raw_block(j, g) + r * 2 + half])
                cot = read_row(lambda half: part[cot_block(j, g) + r * 2 + half])
            store_shifted(gslab, g, holder * 2 + r, cot.astype(F32))
            return 0

        lax.fori_loop(0, 8, rows, 0, unroll=2)
    frame_stats(x, 4, sums, mean, inv_std, ones)

    def normed(g, _):
        norm_silu_frame(
            x, g, mean[pl.ds(g, 1), :], inv_std[pl.ds(g, 1), :],
            gain[0:1, :], bias[0:1, :], slab, g, None,
        )
        return 0

    lax.fori_loop(0, 4, normed, 0)
    wait_weights(weight, taps, sems, 0)
    start_weights(weight, taps, sems, 1)

    def forward(f, _):
        low = jnp.maximum(0, 4 - j - f)
        n = jnp.minimum(2, 7 - j - f) - low + 1
        by_count(conv_taps, slab, f + low - 4 + j, taps.at[0], low, n, acc, f)
        return 0

    lax.fori_loop(0, 5, forward, 0)
    acc[8, 0:8] = mean[...]
    acc[8, 8:16] = inv_std[...]
    acc[8, COLS : COLS + CELLS] = x[j].astype(F32)
    saves = share_copies(acc, acc_out, save_sems)
    saves[0].start()
    saves[1].start()
    wait_weights(weight, taps, sems, 1)

    def backward(f, _):
        low = jnp.maximum(0, f + j - 1)
        by_count(adjoint_taps, gslab, j + f + 2 - low, taps.at[1], low, 3 - low, acc, 5 + f)
        return 0

    lax.fori_loop(0, 3, backward, 0)

    @pl.when(j >= 2)
    def _():
        for n in range(2):
            h[n] = acc[1 + n, COLS : COLS + CELLS, :].astype(BF16)
        frame_stats(h, 2, sums, mean, inv_std, ones)

        def normed1(n, _):
            norm_silu_frame(
                h, n, mean[pl.ds(n, 1), :], inv_std[pl.ds(n, 1), :],
                gain[1:2, :], bias[1:2, :], slab, n, None,
            )
            return 0

        lax.fori_loop(0, 2, normed1, 0)
        by_count(conv_taps, slab, 3 - j, taps.at[1], 4 - j, j - 1, acc, 9)

    saves[2].start()
    saves[3].start()
    for save in saves:
        save.wait()


def rest_kernel(
    table, recv, acc_in, gain, bias, weight, out,
    taps, x, slab, gslab, acc, share, h, sums, mean, inv_std, ones, sems, load_sems,
):
    start_weights(weight, taps, sems, 0)
    loads = share_copies(acc_in, share, load_sems)
    j = lax.axis_index("space")
    has_prev = (table[0, 3] >= 0).astype(F32)
    ones[...] = group_matrix()

    def rows(t, _):
        g, row = t // 8, lax.rem(t, 8)
        block = (g * 2 + lax.rem(row, 2)) * 2
        x[g, pl.ds(row * COLS, COLS), :] = read_row(lambda half: recv[(block + half) * 4 + row // 2])
        return 0

    def cot_rows(t, _):
        g, row = t // 8, lax.rem(t, 8)
        block = 16 + (g * 2 + lax.rem(row, 2)) * 2
        cot = read_row(lambda half: recv[(block + half) * 4 + row // 2])
        store_shifted(gslab, g, row, cot.astype(F32))
        return 0

    lax.fori_loop(0, 32, rows, 0, unroll=4)
    frame_stats(x, 4, sums, mean, inv_std, ones)
    start_weights(weight, taps, sems, 1)

    def normed(g, _):
        mask = jnp.where(g >= j, has_prev, 1.0)

        @pl.when(g != j - 1)
        def _():
            norm_silu_frame(
                x, g, mean[pl.ds(g, 1), :], inv_std[pl.ds(g, 1), :],
                gain[0:1, :], bias[0:1, :], slab, g, mask,
            )

        return 0

    lax.fori_loop(0, 4, normed, 0)
    def cot_frame(g, _):
        lax.fori_loop(0, 8, lambda r, _: cot_rows(g * 8 + r, 0), 0, unroll=4)
        return 0

    lax.fori_loop(0, j + 1, cot_frame, 0)
    acc[...] = jnp.zeros_like(acc)
    wait_weights(weight, taps, sems, 0)
    for load in loads:
        load.start()

    def forward(f, _):
        prev = f < 4 - j
        low = jnp.where(prev, 0, jnp.maximum(0, 8 - j - f))
        n = jnp.where(prev, jnp.minimum(2, 3 - j - f), 2) - low + 1
        first = jnp.where(prev, j + f, f + low - 8 + j)
        by_count(conv_taps, slab, first, taps.at[0], low, n, acc, f)
        return 0

    lax.fori_loop(0, 5, forward, 0)
    wait_weights(weight, taps, sems, 1)

    def backward(f, _):
        n = jnp.minimum(2, f + j - 2) + 1
        by_count(adjoint_taps, gslab, f - 2 + j, taps.at[1], 0, n, acc, 5 + f)
        return 0

    lax.fori_loop(0, 3, backward, 0)

    for load in loads:
        load.wait()

    def rounded(f, _):
        inner = pl.ds(COLS, CELLS)
        h[f] = (acc[f, inner, :] + share[f, inner, :]).astype(BF16)
        return 0

    lax.fori_loop(0, 5, rounded, 0)
    frame_stats(h, 5, sums, mean, inv_std, ones)
    gain1, bias1 = gain[1:2, :], bias[1:2, :]

    def normed1(f, _):
        mask = jnp.where(j - 2 + f < 0, has_prev, 1.0)
        norm_silu_frame(
            h, f, mean[pl.ds(f, 1), :], inv_std[pl.ds(f, 1), :], gain1, bias1, slab, f, mask
        )
        return 0

    lax.fori_loop(0, jnp.minimum(3, 4 - j), normed1, 0)
    by_count(conv_taps, slab, 0, taps.at[1], 0, jnp.minimum(3, 4 - j), acc, 8)
    for i in range(4):
        inner = pl.ds(COLS + i * 64, 64)
        out[i, 0] = (acc[8, inner, :] + share[9, inner, :]).astype(BF16)

    sums[...] = jnp.zeros_like(sums)

    def back_sums(f, _):
        n = f + 2
        one, two = norm_back_sums(
            h, n, mean[pl.ds(n, 1), :], inv_std[pl.ds(n, 1), :], gain1, bias1, acc, 5 + f, share
        )
        sums[pl.ds(f, 1), :] = one
        sums[pl.ds(f + 4, 1), :] = two
        return 0

    lax.fori_loop(0, 3, back_sums, 0)
    sums[...] = group_mean(sums[...], ones)

    def back_rows(t, _):
        f, r = t // 8, lax.rem(t, 8)
        n = f + 2
        g1 = norm_back_row(
            h, n, r, mean[pl.ds(n, 1), :], inv_std[pl.ds(n, 1), :], acc, 5 + f,
            sums[pl.ds(f, 1), :], sums[pl.ds(f + 4, 1), :],
        )
        store_shifted(slab, f, r, g1)
        return 0

    lax.fori_loop(0, 24, back_rows, 0, unroll=4)
    adjoint_taps(slab, 2, taps.at[0], 0, 3, acc, 9)

    m0, i0 = share[8, pl.ds(j, 1), :], share[8, pl.ds(8 + j, 1), :]
    raw_own = share.at[8:9, COLS : COLS + CELLS]
    one, two = norm_back_sums(raw_own, 0, m0, i0, gain[0:1, :], bias[0:1, :], acc, 9, None)
    sums[0:1, :] = one
    sums[1:2, :] = two
    sums[...] = group_mean(sums[...], ones)
    for r in range(8):
        g0 = norm_back_row(raw_own, 0, r, m0, i0, acc, 9, sums[0:1, :], sums[1:2, :])
        out[r // 2, 1, (r % 2) * COLS : (r % 2 + 1) * COLS, :] = g0.astype(BF16)


def per_device(frames, stretch_table, conv_weight, norm_gain, norm_bias, cotangent):
    small = pltpu.CompilerParams(vmem_limit_bytes=8 * 2**20)
    params = pltpu.CompilerParams(vmem_limit_bytes=115 * 2**19)
    weight = conv_weight.reshape(2, 27, C, C)
    mine, mine_cot = frames.reshape(16, 16, C), cotangent.reshape(16, 16, C)
    pieces, *windows = pl.pallas_call(
        prepare_kernel,
        out_shape=[jax.ShapeDtypeStruct((32, 56, 128), BF16)]
        + [jax.ShapeDtypeStruct((28, 16, C), BF16)] * 3,
        in_specs=[SMEM, VMEM, VMEM],
        out_specs=[VMEM] * 4,
        name="prepare",
    )(stretch_table, mine, mine_cot)
    shifted = [
        lax.ppermute(window, "space", [(i, (i + k) % 4) for i in range(4)])
        for k, window in zip((1, 2, 3), windows)
    ]
    spread = lax.all_to_all(pieces, "stretch", 0, 0, tiled=True)
    routed = pl.pallas_call(
        route_kernel,
        out_shape=jax.ShapeDtypeStruct((128, 16, C), BF16),
        in_specs=[VMEM],
        out_specs=HBM,
        scratch_shapes=[
            pltpu.VMEM((33, 16, C), BF16),
            pltpu.VMEM((8, 128), jnp.int32),
            pltpu.SMEM((8, 128), jnp.int32),
            pltpu.VMEM((128, 16, C), BF16),
            pltpu.SemaphoreType.DMA,
            pltpu.SemaphoreType.DMA((4,)),
        ],
        compiler_params=small,
        name="route",
    )(spread)
    recv = lax.all_to_all(routed, ("stretch", "space"), 0, 0, tiled=True)
    acc = pl.pallas_call(
        own_kernel,
        out_shape=jax.ShapeDtypeStruct((32, PADDED, C), F32),
        in_specs=[SMEM] + [VMEM] * 7 + [ANY],
        out_specs=HBM,
        scratch_shapes=[
            pltpu.VMEM((2, 27, C, C), BF16),
            pltpu.VMEM((4, CELLS, C), BF16),
            pltpu.VMEM((4, CELLS, 3 * C), BF16),
            pltpu.VMEM((4, CELLS, 3 * C), BF16),
            pltpu.VMEM((10, PADDED, C), F32),
            pltpu.VMEM((2, CELLS, C), BF16),
            pltpu.VMEM((8, C), F32),
            pltpu.VMEM((8, C), F32),
            pltpu.VMEM((8, C), F32),
            pltpu.VMEM((C, C), BF16),
            pltpu.SemaphoreType.DMA((2, 3)),
            pltpu.SemaphoreType.DMA((4,)),
        ],
        compiler_params=params,
        cost_estimate=pl.CostEstimate(
            flops=1500 * 2 * CELLS * 9 * C * C, bytes_accessed=24 * 2**20, transcendentals=0
        ),
        name="own",
    )(stretch_table, mine, mine_cot, *shifted, norm_gain, norm_bias, weight)
    out = pl.pallas_call(
        rest_kernel,
        out_shape=jax.ShapeDtypeStruct((4, 2, 64, C), BF16),
        in_specs=[SMEM, VMEM, HBM, VMEM, VMEM, ANY],
        out_specs=VMEM,
        scratch_shapes=[
            pltpu.VMEM((2, 27, C, C), BF16),
            pltpu.VMEM((4, CELLS, C), BF16),
            pltpu.VMEM((4, CELLS, 3 * C), BF16),
            pltpu.VMEM((4, CELLS, 3 * C), BF16),
            pltpu.VMEM((10, PADDED, C), F32),
            pltpu.VMEM((10, PADDED, C), F32),
            pltpu.VMEM((5, CELLS, C), BF16),
            pltpu.VMEM((8, C), F32),
            pltpu.VMEM((8, C), F32),
            pltpu.VMEM((8, C), F32),
            pltpu.VMEM((C, C), BF16),
            pltpu.SemaphoreType.DMA((2, 3)),
            pltpu.SemaphoreType.DMA((4,)),
        ],
        compiler_params=pltpu.CompilerParams(vmem_limit_bytes=48 * 2**20),
        cost_estimate=pl.CostEstimate(
            flops=18 * 2 * CELLS * 9 * C * C, bytes_accessed=24 * 2**20, transcendentals=0
        ),
        name="rest",
    )(stretch_table, recv, acc, norm_gain, norm_bias, weight)
    back = lax.all_to_all(out, "space", 0, 0, tiled=True)
    shape = frames.shape
    return back[:, 0].reshape(shape), back[:, 1].reshape(shape)


def solution(mesh):
    in_specs = (
        P("stretch", "space", None, None),
        P("stretch", None),
        P(),
        P(),
        P(),
        P("stretch", "space", None, None),
    )
    out_specs = (P("stretch", "space", None, None), P("stretch", "space", None, None))
    return jax.shard_map(
        per_device, mesh=mesh, in_specs=in_specs, out_specs=out_specs, check_vma=False
    )
```

```python
import jax
import jax.numpy as jnp
from jax import lax
from jax.experimental import pallas as pl
from jax.experimental.pallas import tpu as pltpu
from jax.sharding import PartitionSpec as P

C = 384
GROUPS = 32
GSIZE = C // GROUPS
COLS = 32
ROWS = 8
CELLS = ROWS * COLS
PADDED = CELLS + 2 * COLS
COUNT = float(CELLS * GSIZE)
F32 = jnp.float32
BF16 = jnp.bfloat16
VMEM = pl.BlockSpec(memory_space=pltpu.VMEM)
SMEM = pl.BlockSpec(memory_space=pltpu.SMEM)
HBM = pl.BlockSpec(memory_space=pltpu.HBM)
ANY = pl.BlockSpec(memory_space=pl.ANY)


def group_matrix():
    row = lax.broadcasted_iota(jnp.int32, (C, C), 0) // GSIZE
    col = lax.broadcasted_iota(jnp.int32, (C, C), 1) // GSIZE
    return (row == col).astype(BF16)


def group_mean(sums, ones):
    n = sums.shape[0]
    high = sums.astype(BF16)
    rest = sums - high.astype(F32)
    mid = rest.astype(BF16)
    low = (rest - mid.astype(F32)).astype(BF16)
    parts = jnp.dot(
        jnp.concatenate([high.astype(F32), mid.astype(F32), low.astype(F32)], axis=0).astype(BF16),
        ones[...],
        preferred_element_type=F32,
    )
    return (parts[:n] + parts[n : 2 * n] + parts[2 * n :]) * (1.0 / COUNT)


def fold(values):
    return jnp.sum(values.reshape(COLS // 8, 8, C), axis=0)


def sigmoid(v):
    return 0.5 * jnp.tanh(0.5 * v) + 0.5


def store_shifted(slab, idx, row, values):
    col = lax.broadcasted_iota(jnp.int32, (COLS, C), 0)
    left = jnp.where(col == 0, 0.0, pltpu.roll(values, 1, 0))
    right = jnp.where(col == COLS - 1, 0.0, pltpu.roll(values, COLS - 1, 0))
    at = pl.ds(row * COLS, COLS)
    slab[idx, at, 0:C] = left.astype(BF16)
    slab[idx, at, C : 2 * C] = values.astype(BF16)
    slab[idx, at, 2 * C : 3 * C] = right.astype(BF16)


def conv_taps(slab, first, taps, a, n, acc, f):
    cells = jnp.concatenate([slab[first + i] for i in range(n)], axis=1)
    w = jnp.concatenate(
        [
            jnp.concatenate(
                [taps[pl.ds((a + i) * 9 + 3 * b, 3)].reshape(3 * C, C) for b in range(3)], axis=1
            )
            for i in range(n)
        ],
        axis=0,
    )
    y = jnp.dot(cells, w, preferred_element_type=F32)
    for b in range(3):
        acc[f, (2 - b) * COLS : (2 - b) * COLS + CELLS, :] += y[:, b * C : (b + 1) * C]


def adjoint_taps(slab, first, taps, a, n, acc, f):
    cells = jnp.concatenate([slab[first - i] for i in range(n)], axis=1)
    w = jnp.concatenate(
        [
            jnp.concatenate(
                [taps[(a + i) * 9 + 3 * b + 2 - e] for i in range(n) for e in range(3)], axis=1
            )
            for b in range(3)
        ],
        axis=0,
    )
    y = lax.dot_general(cells, w, (((1,), (1,)), ((), ())), preferred_element_type=F32)
    for b in range(3):
        acc[f, b * COLS : b * COLS + CELLS, :] += y[:, b * C : (b + 1) * C]


def by_count(step, slab, first, taps, a, n, acc, f, beside=None):
    for count in (1, 2, 3):

        @pl.when(n == count)
        def _(count=count):
            step(slab, first, taps, a, count, acc, f)
            if beside is not None:
                beside()


def frame_sums(x, idx):
    def body(r, tot):
        return tot + fold(x[idx, pl.ds(r * COLS, COLS), :].astype(F32))

    tot = lax.fori_loop(0, ROWS, body, jnp.zeros((8, C), F32), unroll=True)
    return jnp.sum(tot, axis=0, keepdims=True)


def frame_square_sums(x, idx, mean):
    def body(r, tot):
        diff = x[idx, pl.ds(r * COLS, COLS), :].astype(F32) - mean
        return tot + fold(diff * diff)

    tot = lax.fori_loop(0, ROWS, body, jnp.zeros((8, C), F32), unroll=True)
    return jnp.sum(tot, axis=0, keepdims=True)


def frame_stats(x, count, sums, mean, inv_std, ones):
    sums[...] = jnp.zeros_like(sums)

    def total(n, _):
        sums[pl.ds(n, 1), :] = frame_sums(x, n)
        return 0

    lax.fori_loop(0, count, total, 0)
    mean[...] = group_mean(sums[...], ones)

    def square(n, _):
        sums[pl.ds(n, 1), :] = frame_square_sums(x, n, mean[pl.ds(n, 1), :])
        return 0

    lax.fori_loop(0, count, square, 0)
    inv_std[...] = lax.rsqrt(group_mean(sums[...], ones) + 1e-5)


def norm_silu_frame(x, idx, mean, inv_std, gain, bias, slab, out_idx, mask):
    scale = inv_std * gain

    def body(r, _):
        v = (x[idx, pl.ds(r * COLS, COLS), :].astype(F32) - mean) * scale + bias
        s = v * sigmoid(v)
        if mask is not None:
            s = s * mask
        store_shifted(slab, out_idx, r, s)
        return 0

    lax.fori_loop(0, ROWS, body, 0, unroll=4)


def norm_back_sums(x, idx, mean, inv_std, gain, bias, acc, f, share):
    def body(r, tot):
        at = pl.ds(COLS + r * COLS, COLS)
        n = (x[idx, pl.ds(r * COLS, COLS), :].astype(F32) - mean) * inv_std
        v = n * gain + bias
        sig = sigmoid(v)
        upstream = acc[f, at, :] if share is None else acc[f, at, :] + share[f, at, :]
        gn = upstream * (sig * (1.0 + v * (1.0 - sig)) * gain)
        acc[f, at, :] = gn
        return tot[0] + fold(gn), tot[1] + fold(gn * n)

    zero = jnp.zeros((8, C), F32)
    one, two = lax.fori_loop(0, ROWS, body, (zero, zero), unroll=True)
    return jnp.sum(one, axis=0, keepdims=True), jnp.sum(two, axis=0, keepdims=True)


def norm_back_row(x, idx, r, mean, inv_std, acc, f, first, second):
    n = (x[idx, pl.ds(r * COLS, COLS), :].astype(F32) - mean) * inv_std
    return inv_std * (acc[f, pl.ds(COLS + r * COLS, COLS), :] - first - n * second)


def read_row(block):
    return jnp.concatenate([block(half) for half in range(2)], axis=0)


def layer_weights(weight, taps, sems, layer):
    return [
        pltpu.make_async_copy(
            weight.at[layer, pl.ds(a * 9, 9)], taps.at[layer, pl.ds(a * 9, 9)], sems.at[layer, a]
        )
        for a in range(3)
    ]


def start_weights(weight, taps, sems, layer):
    for copy in layer_weights(weight, taps, sems, layer):
        copy.start()


def wait_weights(weight, taps, sems, layer):
    for copy in layer_weights(weight, taps, sems, layer):
        copy.wait()


def prepare_kernel(table, frames, cot, pieces, *windows):
    for n, part in enumerate((frames, cot)):
        for c in range(3):
            pieces[n * 16 : n * 16 + 16, c * 16 : c * 16 + 16, :] = part[:, :, c * 128 : c * 128 + 128]
    row = lax.broadcasted_iota(jnp.int32, (8, 128), 0)
    here = lax.broadcasted_iota(jnp.int32, (8, 128), 1) == lax.axis_index("stretch")
    links = jnp.where(row == 0, table[0, 3], jnp.where(row == 1, table[0, 2], 0))
    links = jnp.where(here, links, 0).astype(F32).astype(BF16)
    for k in range(32):
        pieces[k, 48:56, :] = links
    for shift, window in enumerate(windows):
        first = (lax.rem(lax.axis_index("space") + shift + 1, 4) == 0).astype(jnp.int32)
        order = [(frames, g) for g in (3, 0, 1, 2)] + [(cot, g) for g in (3, 2, 1, 0)]
        for n, (part, g) in enumerate(order):

            @pl.when((n >= first) & (n < first + 7))
            def _(n=n, part=part, g=g, first=first, window=window):
                window[pl.ds((n - first) * 4, 4)] = part[g * 4 : g * 4 + 4]


def raw_block(j, g):
    first = (j == 0).astype(jnp.int32)
    return jnp.maximum(lax.rem(g + 1, 4) - first, 0) * 4


def cot_block(j, g):
    first = (j == 0).astype(jnp.int32)
    return jnp.minimum(7 - g - first, 6) * 4


def route_kernel(pieces, out, held, found, links, sorted_blocks, sem, out_sems):
    block = lax.axis_index("stretch")
    g = lax.rem(block, 16) // 4
    raw = block < 16

    found[...] = sum(pieces[k, 48:56, :].astype(F32) for k in range(32)).astype(jnp.int32)
    copy = pltpu.make_async_copy(found, links, sem)
    copy.start()
    for c in range(3):
        held[0:32, :, c * 128 : c * 128 + 128] = pieces[:, c * 16 : c * 16 + 16, :]
    held[32] = jnp.zeros((16, C), BF16)
    copy.wait()

    def body(d, _):
        prv, nxt = links[0, d], links[1, d]
        for j in range(4):
            raw_src = jnp.where(j <= g, prv, jnp.where(j >= g + 2, nxt, -1))
            src = jnp.where(raw, raw_src, jnp.where(j >= g, nxt, -1))
            sorted_blocks[d * 4 + j] = held[jnp.where(src < 0, 32, src)]
        return 0

    sends = []
    for part in range(4):
        lax.fori_loop(part * 8, part * 8 + 8, body, 0, unroll=4)
        at = pl.ds(part * 32, 32)
        sends.append(pltpu.make_async_copy(sorted_blocks.at[at], out.at[at], out_sems.at[part]))
        sends[-1].start()
    for send in sends:
        send.wait()


def share_copies(src, dst, sems):
    inner = pl.ds(COLS, CELLS)
    parts = [(pl.ds(0, 5), inner), (8,), (pl.ds(5, 3), inner), (9, inner)]
    return [
        pltpu.make_async_copy(src.at[part], dst.at[part], sems.at[n])
        for n, part in enumerate(parts)
    ]


def own_kernel(
    table, mine, mine_cot, from1, from2, from3, gain, bias, weight, acc_out,
    taps, x, slab, gslab, acc, h, sums, mean, inv_std, ones, sems, save_sems,
):
    start_weights(weight, taps, sems, 0)
    j = lax.axis_index("space")
    ones[...] = group_matrix()
    acc[...] = jnp.zeros_like(acc)
    for shift, part in enumerate((None, from1, from2, from3)):
        holder = lax.rem(j + 4 - shift, 4)

        def rows(t, _, part=part, holder=holder):
            g, r = t // 2, lax.rem(t, 2)
            at = pl.ds((holder * 2 + r) * COLS, COLS)
            if part is None:
                x[g, at, :] = read_row(lambda half: mine[t * 2 + half])
                cot = read_row(lambda half: mine_cot[t * 2 + half])
            else:
                x[g, at, :] = read_row(lambda half: part[raw_block(j, g) + r * 2 + half])
                cot = read_row(lambda half: part[cot_block(j, g) + r * 2 + half])
            store_shifted(gslab, g, holder * 2 + r, cot.astype(F32))
            return 0

        lax.fori_loop(0, 8, rows, 0, unroll=2)
    frame_stats(x, 4, sums, mean, inv_std, ones)

    def normed(g, _):
        norm_silu_frame(
            x, g, mean[pl.ds(g, 1), :], inv_std[pl.ds(g, 1), :],
            gain[0:1, :], bias[0:1, :], slab, g, None,
        )
        return 0

    lax.fori_loop(0, 4, normed, 0)
    wait_weights(weight, taps, sems, 0)
    start_weights(weight, taps, sems, 1)

    def forward(f, _):
        low = jnp.maximum(0, 4 - j - f)
        n = jnp.minimum(2, 7 - j - f) - low + 1
        by_count(conv_taps, slab, f + low - 4 + j, taps.at[0], low, n, acc, f)
        return 0

    lax.fori_loop(0, 5, forward, 0)
    acc[8, 0:8] = mean[...]
    acc[8, 8:16] = inv_std[...]
    acc[8, COLS : COLS + CELLS] = x[j].astype(F32)
    saves = share_copies(acc, acc_out, save_sems)
    saves[0].start()
    saves[1].start()
    wait_weights(weight, taps, sems, 1)

    def backward(f, _):
        low = jnp.maximum(0, f + j - 1)
        by_count(adjoint_taps, gslab, j + f + 2 - low, taps.at[1], low, 3 - low, acc, 5 + f)
        return 0

    lax.fori_loop(0, 3, backward, 0)

    @pl.when(j >= 2)
    def _():
        for n in range(2):
            h[n] = acc[1 + n, COLS : COLS + CELLS, :].astype(BF16)
        frame_stats(h, 2, sums, mean, inv_std, ones)

        def normed1(n, _):
            norm_silu_frame(
                h, n, mean[pl.ds(n, 1), :], inv_std[pl.ds(n, 1), :],
                gain[1:2, :], bias[1:2, :], slab, n, None,
            )
            return 0

        lax.fori_loop(0, 2, normed1, 0)
        by_count(conv_taps, slab, 3 - j, taps.at[1], 4 - j, j - 1, acc, 9)

    saves[2].start()
    saves[3].start()
    for save in saves:
        save.wait()


def rest_kernel(
    table, recv, acc_in, gain, bias, weight, out,
    taps, x, slab, gslab, acc, share, h, sums, mean, inv_std, ones, sems, load_sems,
):
    start_weights(weight, taps, sems, 0)
    loads = share_copies(acc_in, share, load_sems)
    j = lax.axis_index("space")
    has_prev = (table[0, 3] >= 0).astype(F32)
    ones[...] = group_matrix()

    def rows(t, _):
        g, row = t // 8, lax.rem(t, 8)
        block = (g * 2 + lax.rem(row, 2)) * 2
        x[g, pl.ds(row * COLS, COLS), :] = read_row(lambda half: recv[(block + half) * 4 + row // 2])
        return 0

    def cot_rows(t, _):
        g, row = t // 8, lax.rem(t, 8)
        block = 16 + (g * 2 + lax.rem(row, 2)) * 2
        cot = read_row(lambda half: recv[(block + half) * 4 + row // 2])
        store_shifted(gslab, g, row, cot.astype(F32))
        return 0

    lax.fori_loop(0, 32, rows, 0, unroll=4)
    frame_stats(x, 4, sums, mean, inv_std, ones)
    start_weights(weight, taps, sems, 1)

    def normed(g, _):
        mask = jnp.where(g >= j, has_prev, 1.0)

        @pl.when(g != j - 1)
        def _():
            norm_silu_frame(
                x, g, mean[pl.ds(g, 1), :], inv_std[pl.ds(g, 1), :],
                gain[0:1, :], bias[0:1, :], slab, g, mask,
            )

        return 0

    lax.fori_loop(0, 4, normed, 0)
    def cot_frame(g, _):
        lax.fori_loop(0, 8, lambda r, _: cot_rows(g * 8 + r, 0), 0, unroll=4)
        return 0

    lax.fori_loop(0, j + 1, cot_frame, 0)
    acc[...] = jnp.zeros_like(acc)
    wait_weights(weight, taps, sems, 0)
    for load in loads:
        load.start()

    def forward(f, _):
        prev = f < 4 - j
        low = jnp.where(prev, 0, jnp.maximum(0, 8 - j - f))
        n = jnp.where(prev, jnp.minimum(2, 3 - j - f), 2) - low + 1
        first = jnp.where(prev, j + f, f + low - 8 + j)
        by_count(conv_taps, slab, first, taps.at[0], low, n, acc, f)
        return 0

    lax.fori_loop(0, 5, forward, 0)
    wait_weights(weight, taps, sems, 1)

    def backward(f, _):
        n = jnp.minimum(2, f + j - 2) + 1
        by_count(adjoint_taps, gslab, f - 2 + j, taps.at[1], 0, n, acc, 5 + f)
        return 0

    lax.fori_loop(0, 3, backward, 0)

    for load in loads:
        load.wait()

    def rounded(f, _):
        inner = pl.ds(COLS, CELLS)
        h[f] = (acc[f, inner, :] + share[f, inner, :]).astype(BF16)
        return 0

    lax.fori_loop(0, 5, rounded, 0)
    frame_stats(h, 5, sums, mean, inv_std, ones)
    gain1, bias1 = gain[1:2, :], bias[1:2, :]

    def normed1(f, _):
        mask = jnp.where(j - 2 + f < 0, has_prev, 1.0)
        norm_silu_frame(
            h, f, mean[pl.ds(f, 1), :], inv_std[pl.ds(f, 1), :], gain1, bias1, slab, f, mask
        )
        return 0

    lax.fori_loop(0, jnp.minimum(3, 4 - j), normed1, 0)

    def norm_back():
        sums[...] = jnp.zeros_like(sums)
        for f in range(3):
            n = f + 2
            one, two = norm_back_sums(
                h, n, mean[n : n + 1, :], inv_std[n : n + 1, :], gain1, bias1, acc, 5 + f, share
            )
            sums[f : f + 1, :] = one
            sums[f + 4 : f + 5, :] = two
        sums[...] = group_mean(sums[...], ones[...])
        for f in range(3):
            n = f + 2
            for r in range(ROWS):
                g1 = norm_back_row(
                    h, n, r, mean[n : n + 1, :], inv_std[n : n + 1, :], acc, 5 + f,
                    sums[f : f + 1, :], sums[f + 4 : f + 5, :],
                )
                store_shifted(gslab, f, r, g1)

    by_count(conv_taps, slab, 0, taps.at[1], 0, jnp.minimum(3, 4 - j), acc, 8, norm_back)
    for i in range(4):
        inner = pl.ds(COLS + i * 64, 64)
        out[i, 0] = (acc[8, inner, :] + share[9, inner, :]).astype(BF16)

    adjoint_taps(gslab, 2, taps.at[0], 0, 3, acc, 9)

    m0, i0 = share[8, pl.ds(j, 1), :], share[8, pl.ds(8 + j, 1), :]
    raw_own = share.at[8:9, COLS : COLS + CELLS]
    one, two = norm_back_sums(raw_own, 0, m0, i0, gain[0:1, :], bias[0:1, :], acc, 9, None)
    sums[0:1, :] = one
    sums[1:2, :] = two
    sums[...] = group_mean(sums[...], ones)
    for r in range(8):
        g0 = norm_back_row(raw_own, 0, r, m0, i0, acc, 9, sums[0:1, :], sums[1:2, :])
        out[r // 2, 1, (r % 2) * COLS : (r % 2 + 1) * COLS, :] = g0.astype(BF16)


def per_device(frames, stretch_table, conv_weight, norm_gain, norm_bias, cotangent):
    small = pltpu.CompilerParams(vmem_limit_bytes=8 * 2**20)
    params = pltpu.CompilerParams(vmem_limit_bytes=115 * 2**19)
    weight = conv_weight.reshape(2, 27, C, C)
    mine, mine_cot = frames.reshape(16, 16, C), cotangent.reshape(16, 16, C)
    pieces, *windows = pl.pallas_call(
        prepare_kernel,
        out_shape=[jax.ShapeDtypeStruct((32, 56, 128), BF16)]
        + [jax.ShapeDtypeStruct((28, 16, C), BF16)] * 3,
        in_specs=[SMEM, VMEM, VMEM],
        out_specs=[VMEM] * 4,
        name="prepare",
    )(stretch_table, mine, mine_cot)
    shifted = [
        lax.ppermute(window, "space", [(i, (i + k) % 4) for i in range(4)])
        for k, window in zip((1, 2, 3), windows)
    ]
    spread = lax.all_to_all(pieces, "stretch", 0, 0, tiled=True)
    routed = pl.pallas_call(
        route_kernel,
        out_shape=jax.ShapeDtypeStruct((128, 16, C), BF16),
        in_specs=[VMEM],
        out_specs=HBM,
        scratch_shapes=[
            pltpu.VMEM((33, 16, C), BF16),
            pltpu.VMEM((8, 128), jnp.int32),
            pltpu.SMEM((8, 128), jnp.int32),
            pltpu.VMEM((128, 16, C), BF16),
            pltpu.SemaphoreType.DMA,
            pltpu.SemaphoreType.DMA((4,)),
        ],
        compiler_params=small,
        name="route",
    )(spread)
    recv = lax.all_to_all(routed, ("stretch", "space"), 0, 0, tiled=True)
    acc = pl.pallas_call(
        own_kernel,
        out_shape=jax.ShapeDtypeStruct((32, PADDED, C), F32),
        in_specs=[SMEM] + [VMEM] * 7 + [ANY],
        out_specs=HBM,
        scratch_shapes=[
            pltpu.VMEM((2, 27, C, C), BF16),
            pltpu.VMEM((4, CELLS, C), BF16),
            pltpu.VMEM((4, CELLS, 3 * C), BF16),
            pltpu.VMEM((4, CELLS, 3 * C), BF16),
            pltpu.VMEM((10, PADDED, C), F32),
            pltpu.VMEM((2, CELLS, C), BF16),
            pltpu.VMEM((8, C), F32),
            pltpu.VMEM((8, C), F32),
            pltpu.VMEM((8, C), F32),
            pltpu.VMEM((C, C), BF16),
            pltpu.SemaphoreType.DMA((2, 3)),
            pltpu.SemaphoreType.DMA((4,)),
        ],
        compiler_params=params,
        cost_estimate=pl.CostEstimate(
            flops=1500 * 2 * CELLS * 9 * C * C, bytes_accessed=24 * 2**20, transcendentals=0
        ),
        name="own",
    )(stretch_table, mine, mine_cot, *shifted, norm_gain, norm_bias, weight)
    out = pl.pallas_call(
        rest_kernel,
        out_shape=jax.ShapeDtypeStruct((4, 2, 64, C), BF16),
        in_specs=[SMEM, VMEM, HBM, VMEM, VMEM, ANY],
        out_specs=VMEM,
        scratch_shapes=[
            pltpu.VMEM((2, 27, C, C), BF16),
            pltpu.VMEM((4, CELLS, C), BF16),
            pltpu.VMEM((4, CELLS, 3 * C), BF16),
            pltpu.VMEM((4, CELLS, 3 * C), BF16),
            pltpu.VMEM((10, PADDED, C), F32),
            pltpu.VMEM((10, PADDED, C), F32),
            pltpu.VMEM((5, CELLS, C), BF16),
            pltpu.VMEM((8, C), F32),
            pltpu.VMEM((8, C), F32),
            pltpu.VMEM((8, C), F32),
            pltpu.VMEM((C, C), BF16),
            pltpu.SemaphoreType.DMA((2, 3)),
            pltpu.SemaphoreType.DMA((4,)),
        ],
        compiler_params=pltpu.CompilerParams(vmem_limit_bytes=48 * 2**20),
        cost_estimate=pl.CostEstimate(
            flops=18 * 2 * CELLS * 9 * C * C, bytes_accessed=24 * 2**20, transcendentals=0
        ),
        name="rest",
    )(stretch_table, recv, acc, norm_gain, norm_bias, weight)
    back = lax.all_to_all(out, "space", 0, 0, tiled=True)
    shape = frames.shape
    return back[:, 0].reshape(shape), back[:, 1].reshape(shape)


def solution(mesh):
    in_specs = (
        P("stretch", "space", None, None),
        P("stretch", None),
        P(),
        P(),
        P(),
        P("stretch", "space", None, None),
    )
    out_specs = (P("stretch", "space", None, None), P("stretch", "space", None, None))
    return jax.shard_map(
        per_device, mesh=mesh, in_specs=in_specs, out_specs=out_specs, check_vma=False
    )
```

```python
import jax
import jax.numpy as jnp
from jax import lax
from jax.experimental import pallas as pl
from jax.experimental.pallas import tpu as pltpu
from jax.sharding import PartitionSpec as P

C = 384
GROUPS = 32
GSIZE = C // GROUPS
COLS = 32
ROWS = 8
CELLS = ROWS * COLS
PADDED = CELLS + 2 * COLS
COUNT = float(CELLS * GSIZE)
F32 = jnp.float32
BF16 = jnp.bfloat16
VMEM = pl.BlockSpec(memory_space=pltpu.VMEM)
SMEM = pl.BlockSpec(memory_space=pltpu.SMEM)
HBM = pl.BlockSpec(memory_space=pltpu.HBM)
ANY = pl.BlockSpec(memory_space=pl.ANY)


def group_matrix():
    row = lax.broadcasted_iota(jnp.int32, (C, C), 0) // GSIZE
    col = lax.broadcasted_iota(jnp.int32, (C, C), 1) // GSIZE
    return (row == col).astype(BF16)


def group_mean(sums, ones):
    n = sums.shape[0]
    high = sums.astype(BF16)
    rest = sums - high.astype(F32)
    mid = rest.astype(BF16)
    low = (rest - mid.astype(F32)).astype(BF16)
    parts = jnp.dot(
        jnp.concatenate([high.astype(F32), mid.astype(F32), low.astype(F32)], axis=0).astype(BF16),
        ones[...],
        preferred_element_type=F32,
    )
    return (parts[:n] + parts[n : 2 * n] + parts[2 * n :]) * (1.0 / COUNT)


def fold(values):
    return jnp.sum(values.reshape(COLS // 8, 8, C), axis=0)


def sigmoid(v):
    return 0.5 * jnp.tanh(0.5 * v) + 0.5


def store_shifted(slab, idx, row, values):
    col = lax.broadcasted_iota(jnp.int32, (COLS, C), 0)
    left = jnp.where(col == 0, 0.0, pltpu.roll(values, 1, 0))
    right = jnp.where(col == COLS - 1, 0.0, pltpu.roll(values, COLS - 1, 0))
    at = pl.ds(row * COLS, COLS)
    slab[idx, at, 0:C] = left.astype(BF16)
    slab[idx, at, C : 2 * C] = values.astype(BF16)
    slab[idx, at, 2 * C : 3 * C] = right.astype(BF16)


def conv_taps(slab, first, taps, a, n, acc, f):
    cells = jnp.concatenate([slab[first + i] for i in range(n)], axis=1)
    w = jnp.concatenate(
        [
            jnp.concatenate(
                [taps[pl.ds((a + i) * 9 + 3 * b, 3)].reshape(3 * C, C) for b in range(3)], axis=1
            )
            for i in range(n)
        ],
        axis=0,
    )
    y = jnp.dot(cells, w, preferred_element_type=F32)
    for b in range(3):
        acc[f, (2 - b) * COLS : (2 - b) * COLS + CELLS, :] += y[:, b * C : (b + 1) * C]


def adjoint_taps(slab, first, taps, a, n, acc, f):
    cells = jnp.concatenate([slab[first - i] for i in range(n)], axis=1)
    w = jnp.concatenate(
        [
            jnp.concatenate(
                [taps[(a + i) * 9 + 3 * b + 2 - e] for i in range(n) for e in range(3)], axis=1
            )
            for b in range(3)
        ],
        axis=0,
    )
    y = lax.dot_general(cells, w, (((1,), (1,)), ((), ())), preferred_element_type=F32)
    for b in range(3):
        acc[f, b * COLS : b * COLS + CELLS, :] += y[:, b * C : (b + 1) * C]


def by_count(step, slab, first, taps, a, n, acc, f, beside=None, most=3):
    for count in range(1, most + 1):

        @pl.when(n == count)
        def _(count=count):
            step(slab, first, taps, a, count, acc, f)
            if beside is not None:
                beside()


def frame_sums(x, idx):
    def body(r, tot):
        return tot + fold(x[idx, pl.ds(r * COLS, COLS), :].astype(F32))

    tot = lax.fori_loop(0, ROWS, body, jnp.zeros((8, C), F32), unroll=True)
    return jnp.sum(tot, axis=0, keepdims=True)


def frame_square_sums(x, idx, mean):
    def body(r, tot):
        diff = x[idx, pl.ds(r * COLS, COLS), :].astype(F32) - mean
        return tot + fold(diff * diff)

    tot = lax.fori_loop(0, ROWS, body, jnp.zeros((8, C), F32), unroll=True)
    return jnp.sum(tot, axis=0, keepdims=True)


def frame_stats(x, count, sums, mean, inv_std, ones, straight=False):
    sums[...] = jnp.zeros_like(sums)
    unroll = count if straight else 1

    def total(n, _):
        sums[pl.ds(n, 1), :] = frame_sums(x, n)
        return 0

    lax.fori_loop(0, count, total, 0, unroll=unroll)
    mean[...] = group_mean(sums[...], ones)

    def square(n, _):
        sums[pl.ds(n, 1), :] = frame_square_sums(x, n, mean[pl.ds(n, 1), :])
        return 0

    lax.fori_loop(0, count, square, 0, unroll=unroll)
    inv_std[...] = lax.rsqrt(group_mean(sums[...], ones) + 1e-5)


def norm_silu_frame(x, idx, mean, inv_std, gain, bias, slab, out_idx, mask):
    scale = inv_std * gain

    def body(r, _):
        v = (x[idx, pl.ds(r * COLS, COLS), :].astype(F32) - mean) * scale + bias
        s = v * sigmoid(v)
        if mask is not None:
            s = s * mask
        store_shifted(slab, out_idx, r, s)
        return 0

    lax.fori_loop(0, ROWS, body, 0, unroll=4)


def norm_back_sums(x, idx, mean, inv_std, gain, bias, acc, f, share):
    def body(r, tot):
        at = pl.ds(COLS + r * COLS, COLS)
        n = (x[idx, pl.ds(r * COLS, COLS), :].astype(F32) - mean) * inv_std
        v = n * gain + bias
        sig = sigmoid(v)
        upstream = acc[f, at, :] if share is None else acc[f, at, :] + share[f, at, :]
        gn = upstream * (sig * (1.0 + v * (1.0 - sig)) * gain)
        acc[f, at, :] = gn
        return tot[0] + fold(gn), tot[1] + fold(gn * n)

    zero = jnp.zeros((8, C), F32)
    one, two = lax.fori_loop(0, ROWS, body, (zero, zero), unroll=True)
    return jnp.sum(one, axis=0, keepdims=True), jnp.sum(two, axis=0, keepdims=True)


def norm_back_row(x, idx, r, mean, inv_std, acc, f, first, second):
    n = (x[idx, pl.ds(r * COLS, COLS), :].astype(F32) - mean) * inv_std
    return inv_std * (acc[f, pl.ds(COLS + r * COLS, COLS), :] - first - n * second)


def read_row(block):
    return jnp.concatenate([block(half) for half in range(2)], axis=0)


def layer_weights(weight, taps, sems, layer):
    return [
        pltpu.make_async_copy(
            weight.at[layer, pl.ds(a * 9, 9)], taps.at[layer, pl.ds(a * 9, 9)], sems.at[layer, a]
        )
        for a in range(3)
    ]


def start_weights(weight, taps, sems, layer):
    for copy in layer_weights(weight, taps, sems, layer):
        copy.start()


def wait_weights(weight, taps, sems, layer):
    for copy in layer_weights(weight, taps, sems, layer):
        copy.wait()


def prepare_kernel(table, frames, cot, pieces, *windows):
    for n, part in enumerate((frames, cot)):
        for c in range(3):
            pieces[n * 16 : n * 16 + 16, c * 16 : c * 16 + 16, :] = part[:, :, c * 128 : c * 128 + 128]
    row = lax.broadcasted_iota(jnp.int32, (8, 128), 0)
    here = lax.broadcasted_iota(jnp.int32, (8, 128), 1) == lax.axis_index("stretch")
    links = jnp.where(row == 0, table[0, 3], jnp.where(row == 1, table[0, 2], 0))
    links = jnp.where(here, links, 0).astype(F32).astype(BF16)
    for k in range(32):
        pieces[k, 48:56, :] = links
    for shift, window in enumerate(windows):
        first = (lax.rem(lax.axis_index("space") + shift + 1, 4) == 0).astype(jnp.int32)
        order = [(frames, g) for g in (3, 0, 1, 2)] + [(cot, g) for g in (3, 2, 1, 0)]
        for n, (part, g) in enumerate(order):

            @pl.when((n >= first) & (n < first + 7))
            def _(n=n, part=part, g=g, first=first, window=window):
                window[pl.ds((n - first) * 4, 4)] = part[g * 4 : g * 4 + 4]


def raw_block(j, g):
    first = (j == 0).astype(jnp.int32)
    return jnp.maximum(lax.rem(g + 1, 4) - first, 0) * 4


def cot_block(j, g):
    first = (j == 0).astype(jnp.int32)
    return jnp.minimum(7 - g - first, 6) * 4


def route_kernel(pieces, out, held, found, links, sorted_blocks, sem, out_sems):
    block = lax.axis_index("stretch")
    g = lax.rem(block, 16) // 4
    raw = block < 16

    found[...] = sum(pieces[k, 48:56, :].astype(F32) for k in range(32)).astype(jnp.int32)
    copy = pltpu.make_async_copy(found, links, sem)
    copy.start()
    for c in range(3):
        held[0:32, :, c * 128 : c * 128 + 128] = pieces[:, c * 16 : c * 16 + 16, :]
    held[32] = jnp.zeros((16, C), BF16)
    copy.wait()

    def body(d, _):
        prv, nxt = links[0, d], links[1, d]
        for j in range(4):
            raw_src = jnp.where(j <= g, prv, jnp.where(j >= g + 2, nxt, -1))
            src = jnp.where(raw, raw_src, jnp.where(j >= g, nxt, -1))
            sorted_blocks[d * 4 + j] = held[jnp.where(src < 0, 32, src)]
        return 0

    sends = []
    for part in range(4):
        lax.fori_loop(part * 8, part * 8 + 8, body, 0, unroll=4)
        at = pl.ds(part * 32, 32)
        sends.append(pltpu.make_async_copy(sorted_blocks.at[at], out.at[at], out_sems.at[part]))
        sends[-1].start()
    for send in sends:
        send.wait()


def share_copies(src, dst, sems):
    inner = pl.ds(COLS, CELLS)
    parts = [(pl.ds(0, 5), inner), (8,), (pl.ds(5, 3), inner), (9, inner)]
    return [
        pltpu.make_async_copy(src.at[part], dst.at[part], sems.at[n])
        for n, part in enumerate(parts)
    ]


def own_kernel(
    table, mine, mine_cot, from1, from2, from3, gain, bias, weight, acc_out,
    taps, x, slab, gslab, acc, h, sums, mean, inv_std, ones, sems, save_sems,
):
    start_weights(weight, taps, sems, 0)
    j = lax.axis_index("space")
    ones[...] = group_matrix()
    acc[...] = jnp.zeros_like(acc)
    for shift, part in enumerate((None, from1, from2, from3)):
        holder = lax.rem(j + 4 - shift, 4)

        def rows(t, _, part=part, holder=holder):
            g, r = t // 2, lax.rem(t, 2)
            at = pl.ds((holder * 2 + r) * COLS, COLS)
            if part is None:
                x[g, at, :] = read_row(lambda half: mine[t * 2 + half])
                cot = read_row(lambda half: mine_cot[t * 2 + half])
            else:
                x[g, at, :] = read_row(lambda half: part[raw_block(j, g) + r * 2 + half])
                cot = read_row(lambda half: part[cot_block(j, g) + r * 2 + half])
            store_shifted(gslab, g, holder * 2 + r, cot.astype(F32))
            return 0

        lax.fori_loop(0, 8, rows, 0, unroll=2)
    frame_stats(x, 4, sums, mean, inv_std, ones)

    def normed(g, _):
        norm_silu_frame(
            x, g, mean[pl.ds(g, 1), :], inv_std[pl.ds(g, 1), :],
            gain[0:1, :], bias[0:1, :], slab, g, None,
        )
        return 0

    lax.fori_loop(0, 4, normed, 0)
    wait_weights(weight, taps, sems, 0)
    start_weights(weight, taps, sems, 1)

    def forward(f, _):
        low = jnp.maximum(0, 4 - j - f)
        n = jnp.minimum(2, 7 - j - f) - low + 1
        by_count(conv_taps, slab, f + low - 4 + j, taps.at[0], low, n, acc, f)
        return 0

    lax.fori_loop(0, 5, forward, 0)
    acc[8, 0:8] = mean[...]
    acc[8, 8:16] = inv_std[...]
    acc[8, COLS : COLS + CELLS] = x[j].astype(F32)
    saves = share_copies(acc, acc_out, save_sems)
    saves[0].start()
    saves[1].start()
    wait_weights(weight, taps, sems, 1)

    def backward(f, _):
        low = jnp.maximum(0, f + j - 1)
        by_count(adjoint_taps, gslab, j + f + 2 - low, taps.at[1], low, 3 - low, acc, 5 + f)
        return 0

    lax.fori_loop(0, 3, backward, 0)

    @pl.when(j >= 2)
    def _():
        for n in range(2):
            h[n] = acc[1 + n, COLS : COLS + CELLS, :].astype(BF16)
        frame_stats(h, 2, sums, mean, inv_std, ones)

        def normed1(n, _):
            norm_silu_frame(
                h, n, mean[pl.ds(n, 1), :], inv_std[pl.ds(n, 1), :],
                gain[1:2, :], bias[1:2, :], slab, n, None,
            )
            return 0

        lax.fori_loop(0, 2, normed1, 0)
        by_count(conv_taps, slab, 3 - j, taps.at[1], 4 - j, j - 1, acc, 9, most=2)

    saves[2].start()
    saves[3].start()
    for save in saves:
        save.wait()


def rest_kernel(
    table, recv, acc_in, gain, bias, weight, out,
    taps, x, slab, gslab, acc, share, h, sums, mean, inv_std, ones, sems, load_sems,
):
    start_weights(weight, taps, sems, 0)
    loads = share_copies(acc_in, share, load_sems)
    j = lax.axis_index("space")
    has_prev = (table[0, 3] >= 0).astype(F32)
    ones[...] = group_matrix()

    def rows(t, _):
        g, row = t // 8, lax.rem(t, 8)
        block = (g * 2 + lax.rem(row, 2)) * 2
        x[g, pl.ds(row * COLS, COLS), :] = read_row(lambda half: recv[(block + half) * 4 + row // 2])
        return 0

    def cot_rows(t, _):
        g, row = t // 8, lax.rem(t, 8)
        block = 16 + (g * 2 + lax.rem(row, 2)) * 2
        cot = read_row(lambda half: recv[(block + half) * 4 + row // 2])
        store_shifted(gslab, g, row, cot.astype(F32))
        return 0

    lax.fori_loop(0, 32, rows, 0, unroll=4)
    frame_stats(x, 4, sums, mean, inv_std, ones)
    start_weights(weight, taps, sems, 1)

    def normed(g, _):
        mask = jnp.where(g >= j, has_prev, 1.0)

        @pl.when(g != j - 1)
        def _():
            norm_silu_frame(
                x, g, mean[pl.ds(g, 1), :], inv_std[pl.ds(g, 1), :],
                gain[0:1, :], bias[0:1, :], slab, g, mask,
            )

        return 0

    lax.fori_loop(0, 4, normed, 0)
    def cot_frame(g, _):
        lax.fori_loop(0, 8, lambda r, _: cot_rows(g * 8 + r, 0), 0, unroll=4)
        return 0

    lax.fori_loop(0, j + 1, cot_frame, 0)
    acc[...] = jnp.zeros_like(acc)
    wait_weights(weight, taps, sems, 0)
    for load in loads:
        load.start()

    def forward(f, _):
        prev = f < 4 - j
        low = jnp.where(prev, 0, jnp.maximum(0, 8 - j - f))
        n = jnp.where(prev, jnp.minimum(2, 3 - j - f), 2) - low + 1
        first = jnp.where(prev, j + f, f + low - 8 + j)
        by_count(conv_taps, slab, first, taps.at[0], low, n, acc, f)
        return 0

    lax.fori_loop(0, 5, forward, 0)
    wait_weights(weight, taps, sems, 1)

    def layer1_stats():
        inner = pl.ds(COLS, CELLS)
        for f in range(5):
            h[f] = (acc[f, inner, :] + share[f, inner, :]).astype(BF16)
        frame_stats(h, 5, sums, mean, inv_std, ones, straight=True)

    def backward(f, beside=None):
        n = jnp.minimum(2, f + j - 2) + 1
        by_count(adjoint_taps, gslab, f - 2 + j, taps.at[1], 0, n, acc, 5 + f, beside)

    for load in loads:
        load.wait()
    backward(2, layer1_stats)

    def backward_rest(f, _):
        backward(f)
        return 0

    lax.fori_loop(0, 2, backward_rest, 0)
    gain1, bias1 = gain[1:2, :], bias[1:2, :]

    def normed1(f, _):
        mask = jnp.where(j - 2 + f < 0, has_prev, 1.0)
        norm_silu_frame(
            h, f, mean[pl.ds(f, 1), :], inv_std[pl.ds(f, 1), :], gain1, bias1, slab, f, mask
        )
        return 0

    lax.fori_loop(0, jnp.minimum(3, 4 - j), normed1, 0)

    def norm_back():
        sums[...] = jnp.zeros_like(sums)
        for f in range(3):
            n = f + 2
            one, two = norm_back_sums(
                h, n, mean[n : n + 1, :], inv_std[n : n + 1, :], gain1, bias1, acc, 5 + f, share
            )
            sums[f : f + 1, :] = one
            sums[f + 4 : f + 5, :] = two
        sums[...] = group_mean(sums[...], ones[...])
        for f in range(3):
            n = f + 2
            for r in range(ROWS):
                g1 = norm_back_row(
                    h, n, r, mean[n : n + 1, :], inv_std[n : n + 1, :], acc, 5 + f,
                    sums[f : f + 1, :], sums[f + 4 : f + 5, :],
                )
                store_shifted(gslab, f, r, g1)

    by_count(conv_taps, slab, 0, taps.at[1], 0, jnp.minimum(3, 4 - j), acc, 8, norm_back)
    for i in range(4):
        inner = pl.ds(COLS + i * 64, 64)
        out[i, 0] = (acc[8, inner, :] + share[9, inner, :]).astype(BF16)

    adjoint_taps(gslab, 2, taps.at[0], 0, 3, acc, 9)

    m0, i0 = share[8, pl.ds(j, 1), :], share[8, pl.ds(8 + j, 1), :]
    raw_own = share.at[8:9, COLS : COLS + CELLS]
    one, two = norm_back_sums(raw_own, 0, m0, i0, gain[0:1, :], bias[0:1, :], acc, 9, None)
    sums[0:1, :] = one
    sums[1:2, :] = two
    sums[...] = group_mean(sums[...], ones)
    for r in range(8):
        g0 = norm_back_row(raw_own, 0, r, m0, i0, acc, 9, sums[0:1, :], sums[1:2, :])
        out[r // 2, 1, (r % 2) * COLS : (r % 2 + 1) * COLS, :] = g0.astype(BF16)


def per_device(frames, stretch_table, conv_weight, norm_gain, norm_bias, cotangent):
    small = pltpu.CompilerParams(vmem_limit_bytes=8 * 2**20)
    params = pltpu.CompilerParams(vmem_limit_bytes=115 * 2**19)
    weight = conv_weight.reshape(2, 27, C, C)
    mine, mine_cot = frames.reshape(16, 16, C), cotangent.reshape(16, 16, C)
    pieces, *windows = pl.pallas_call(
        prepare_kernel,
        out_shape=[jax.ShapeDtypeStruct((32, 56, 128), BF16)]
        + [jax.ShapeDtypeStruct((28, 16, C), BF16)] * 3,
        in_specs=[SMEM, VMEM, VMEM],
        out_specs=[VMEM] * 4,
        name="prepare",
    )(stretch_table, mine, mine_cot)
    shifted = [
        lax.ppermute(window, "space", [(i, (i + k) % 4) for i in range(4)])
        for k, window in zip((1, 2, 3), windows)
    ]
    spread = lax.all_to_all(pieces, "stretch", 0, 0, tiled=True)
    routed = pl.pallas_call(
        route_kernel,
        out_shape=jax.ShapeDtypeStruct((128, 16, C), BF16),
        in_specs=[VMEM],
        out_specs=HBM,
        scratch_shapes=[
            pltpu.VMEM((33, 16, C), BF16),
            pltpu.VMEM((8, 128), jnp.int32),
            pltpu.SMEM((8, 128), jnp.int32),
            pltpu.VMEM((128, 16, C), BF16),
            pltpu.SemaphoreType.DMA,
            pltpu.SemaphoreType.DMA((4,)),
        ],
        compiler_params=small,
        name="route",
    )(spread)
    recv = lax.all_to_all(routed, ("stretch", "space"), 0, 0, tiled=True)
    acc = pl.pallas_call(
        own_kernel,
        out_shape=jax.ShapeDtypeStruct((32, PADDED, C), F32),
        in_specs=[SMEM] + [VMEM] * 7 + [ANY],
        out_specs=HBM,
        scratch_shapes=[
            pltpu.VMEM((2, 27, C, C), BF16),
            pltpu.VMEM((4, CELLS, C), BF16),
            pltpu.VMEM((4, CELLS, 3 * C), BF16),
            pltpu.VMEM((4, CELLS, 3 * C), BF16),
            pltpu.VMEM((10, PADDED, C), F32),
            pltpu.VMEM((2, CELLS, C), BF16),
            pltpu.VMEM((8, C), F32),
            pltpu.VMEM((8, C), F32),
            pltpu.VMEM((8, C), F32),
            pltpu.VMEM((C, C), BF16),
            pltpu.SemaphoreType.DMA((2, 3)),
            pltpu.SemaphoreType.DMA((4,)),
        ],
        compiler_params=params,
        cost_estimate=pl.CostEstimate(
            flops=1500 * 2 * CELLS * 9 * C * C, bytes_accessed=24 * 2**20, transcendentals=0
        ),
        name="own",
    )(stretch_table, mine, mine_cot, *shifted, norm_gain, norm_bias, weight)
    out = pl.pallas_call(
        rest_kernel,
        out_shape=jax.ShapeDtypeStruct((4, 2, 64, C), BF16),
        in_specs=[SMEM, VMEM, HBM, VMEM, VMEM, ANY],
        out_specs=VMEM,
        scratch_shapes=[
            pltpu.VMEM((2, 27, C, C), BF16),
            pltpu.VMEM((4, CELLS, C), BF16),
            pltpu.VMEM((4, CELLS, 3 * C), BF16),
            pltpu.VMEM((4, CELLS, 3 * C), BF16),
            pltpu.VMEM((10, PADDED, C), F32),
            pltpu.VMEM((10, PADDED, C), F32),
            pltpu.VMEM((5, CELLS, C), BF16),
            pltpu.VMEM((8, C), F32),
            pltpu.VMEM((8, C), F32),
            pltpu.VMEM((8, C), F32),
            pltpu.VMEM((C, C), BF16),
            pltpu.SemaphoreType.DMA((2, 3)),
            pltpu.SemaphoreType.DMA((4,)),
        ],
        compiler_params=pltpu.CompilerParams(vmem_limit_bytes=48 * 2**20),
        cost_estimate=pl.CostEstimate(
            flops=18 * 2 * CELLS * 9 * C * C, bytes_accessed=24 * 2**20, transcendentals=0
        ),
        name="rest",
    )(stretch_table, recv, acc, norm_gain, norm_bias, weight)
    back = lax.all_to_all(out, "space", 0, 0, tiled=True)
    shape = frames.shape
    return back[:, 0].reshape(shape), back[:, 1].reshape(shape)


def solution(mesh):
    in_specs = (
        P("stretch", "space", None, None),
        P("stretch", None),
        P(),
        P(),
        P(),
        P("stretch", "space", None, None),
    )
    out_specs = (P("stretch", "space", None, None), P("stretch", "space", None, None))
    return jax.shard_map(
        per_device, mesh=mesh, in_specs=in_specs, out_specs=out_specs, check_vma=False
    )
```

```python
import jax
import jax.numpy as jnp
from jax import lax
from jax.experimental import pallas as pl
from jax.experimental.pallas import tpu as pltpu
from jax.sharding import PartitionSpec as P

C = 384
GROUPS = 32
GSIZE = C // GROUPS
COLS = 32
ROWS = 8
CELLS = ROWS * COLS
PADDED = CELLS + 2 * COLS
COUNT = float(CELLS * GSIZE)
F32 = jnp.float32
BF16 = jnp.bfloat16
VMEM = pl.BlockSpec(memory_space=pltpu.VMEM)
SMEM = pl.BlockSpec(memory_space=pltpu.SMEM)
HBM = pl.BlockSpec(memory_space=pltpu.HBM)
ANY = pl.BlockSpec(memory_space=pl.ANY)


def group_matrix():
    row = lax.broadcasted_iota(jnp.int32, (C, C), 0) // GSIZE
    col = lax.broadcasted_iota(jnp.int32, (C, C), 1) // GSIZE
    return (row == col).astype(BF16)


def group_mean(sums, ones):
    n = sums.shape[0]
    high = sums.astype(BF16)
    rest = sums - high.astype(F32)
    mid = rest.astype(BF16)
    low = (rest - mid.astype(F32)).astype(BF16)
    parts = jnp.dot(
        jnp.concatenate([high.astype(F32), mid.astype(F32), low.astype(F32)], axis=0).astype(BF16),
        ones[...],
        preferred_element_type=F32,
    )
    return (parts[:n] + parts[n : 2 * n] + parts[2 * n :]) * (1.0 / COUNT)


def fold(values):
    return jnp.sum(values.reshape(COLS // 8, 8, C), axis=0)


def sigmoid(v):
    return 0.5 * jnp.tanh(0.5 * v) + 0.5


def store_shifted(slab, idx, row, values):
    col = lax.broadcasted_iota(jnp.int32, (COLS, C), 0)
    left = jnp.where(col == 0, 0.0, pltpu.roll(values, 1, 0))
    right = jnp.where(col == COLS - 1, 0.0, pltpu.roll(values, COLS - 1, 0))
    at = pl.ds(row * COLS, COLS)
    slab[idx, at, 0:C] = left.astype(BF16)
    slab[idx, at, C : 2 * C] = values.astype(BF16)
    slab[idx, at, 2 * C : 3 * C] = right.astype(BF16)


def conv_taps(slab, first, taps, a, n, acc, f):
    cells = jnp.concatenate([slab[first + i] for i in range(n)], axis=1)
    w = jnp.concatenate(
        [
            jnp.concatenate(
                [taps[pl.ds((a + i) * 9 + 3 * b, 3)].reshape(3 * C, C) for b in range(3)], axis=1
            )
            for i in range(n)
        ],
        axis=0,
    )
    y = jnp.dot(cells, w, preferred_element_type=F32)
    for b in range(3):
        acc[f, (2 - b) * COLS : (2 - b) * COLS + CELLS, :] += y[:, b * C : (b + 1) * C]


def adjoint_taps(slab, first, taps, a, n, acc, f):
    cells = jnp.concatenate([slab[first - i] for i in range(n)], axis=1)
    w = jnp.concatenate(
        [
            jnp.concatenate(
                [taps[(a + i) * 9 + 3 * b + 2 - e] for i in range(n) for e in range(3)], axis=1
            )
            for b in range(3)
        ],
        axis=0,
    )
    y = lax.dot_general(cells, w, (((1,), (1,)), ((), ())), preferred_element_type=F32)
    for b in range(3):
        acc[f, b * COLS : b * COLS + CELLS, :] += y[:, b * C : (b + 1) * C]


def by_count(step, slab, first, taps, a, n, acc, f, beside=None, most=3):
    for count in range(1, most + 1):

        @pl.when(n == count)
        def _(count=count):
            step(slab, first, taps, a, count, acc, f)
            if beside is not None:
                beside()


def frame_sums(x, idx):
    def body(r, tot):
        return tot + fold(x[idx, pl.ds(r * COLS, COLS), :].astype(F32))

    tot = lax.fori_loop(0, ROWS, body, jnp.zeros((8, C), F32), unroll=True)
    return jnp.sum(tot, axis=0, keepdims=True)


def frame_square_sums(x, idx, mean):
    def body(r, tot):
        diff = x[idx, pl.ds(r * COLS, COLS), :].astype(F32) - mean
        return tot + fold(diff * diff)

    tot = lax.fori_loop(0, ROWS, body, jnp.zeros((8, C), F32), unroll=True)
    return jnp.sum(tot, axis=0, keepdims=True)


def frame_stats(x, count, sums, mean, inv_std, ones):
    sums[...] = jnp.zeros_like(sums)

    def total(n, _):
        sums[pl.ds(n, 1), :] = frame_sums(x, n)
        return 0

    lax.fori_loop(0, count, total, 0)
    mean[...] = group_mean(sums[...], ones)

    def square(n, _):
        sums[pl.ds(n, 1), :] = frame_square_sums(x, n, mean[pl.ds(n, 1), :])
        return 0

    lax.fori_loop(0, count, square, 0)
    inv_std[...] = lax.rsqrt(group_mean(sums[...], ones) + 1e-5)


def norm_silu_frame(x, idx, mean, inv_std, gain, bias, slab, out_idx, mask):
    scale = inv_std * gain

    def body(r, _):
        v = (x[idx, pl.ds(r * COLS, COLS), :].astype(F32) - mean) * scale + bias
        s = v * sigmoid(v)
        if mask is not None:
            s = s * mask
        store_shifted(slab, out_idx, r, s)
        return 0

    lax.fori_loop(0, ROWS, body, 0, unroll=4)


def norm_back_sums(x, idx, mean, inv_std, gain, bias, acc, f, share):
    def body(r, tot):
        at = pl.ds(COLS + r * COLS, COLS)
        n = (x[idx, pl.ds(r * COLS, COLS), :].astype(F32) - mean) * inv_std
        v = n * gain + bias
        sig = sigmoid(v)
        upstream = acc[f, at, :] if share is None else acc[f, at, :] + share[f, at, :]
        gn = upstream * (sig * (1.0 + v * (1.0 - sig)) * gain)
        acc[f, at, :] = gn
        return tot[0] + fold(gn), tot[1] + fold(gn * n)

    zero = jnp.zeros((8, C), F32)
    one, two = lax.fori_loop(0, ROWS, body, (zero, zero), unroll=True)
    return jnp.sum(one, axis=0, keepdims=True), jnp.sum(two, axis=0, keepdims=True)


def norm_back_row(x, idx, r, mean, inv_std, acc, f, first, second):
    n = (x[idx, pl.ds(r * COLS, COLS), :].astype(F32) - mean) * inv_std
    return inv_std * (acc[f, pl.ds(COLS + r * COLS, COLS), :] - first - n * second)


def read_row(block):
    return jnp.concatenate([block(half) for half in range(2)], axis=0)


def layer_weights(weight, taps, sems, layer):
    return [
        pltpu.make_async_copy(
            weight.at[layer, pl.ds(a * 9, 9)], taps.at[layer, pl.ds(a * 9, 9)], sems.at[layer, a]
        )
        for a in range(3)
    ]


def start_weights(weight, taps, sems, layer):
    for copy in layer_weights(weight, taps, sems, layer):
        copy.start()


def wait_weights(weight, taps, sems, layer):
    for copy in layer_weights(weight, taps, sems, layer):
        copy.wait()


def prepare_kernel(table, frames, cot, pieces, *windows):
    for n, part in enumerate((frames, cot)):
        for c in range(3):
            pieces[n * 16 : n * 16 + 16, c * 16 : c * 16 + 16, :] = part[:, :, c * 128 : c * 128 + 128]
    row = lax.broadcasted_iota(jnp.int32, (8, 128), 0)
    here = lax.broadcasted_iota(jnp.int32, (8, 128), 1) == lax.axis_index("stretch")
    links = jnp.where(row == 0, table[0, 3], jnp.where(row == 1, table[0, 2], 0))
    links = jnp.where(here, links, 0).astype(F32).astype(BF16)
    for k in range(32):
        pieces[k, 48:56, :] = links
    for shift, window in enumerate(windows):
        first = (lax.rem(lax.axis_index("space") + shift + 1, 4) == 0).astype(jnp.int32)
        order = [(frames, g) for g in (3, 0, 1, 2)] + [(cot, g) for g in (3, 2, 1, 0)]
        for n, (part, g) in enumerate(order):

            @pl.when((n >= first) & (n < first + 7))
            def _(n=n, part=part, g=g, first=first, window=window):
                window[pl.ds((n - first) * 4, 4)] = part[g * 4 : g * 4 + 4]


def raw_block(j, g):
    first = (j == 0).astype(jnp.int32)
    return jnp.maximum(lax.rem(g + 1, 4) - first, 0) * 4


def cot_block(j, g):
    first = (j == 0).astype(jnp.int32)
    return jnp.minimum(7 - g - first, 6) * 4


def route_kernel(pieces, out, held, found, links, sorted_blocks, sem, out_sems):
    block = lax.axis_index("stretch")
    g = lax.rem(block, 16) // 4
    raw = block < 16

    found[...] = sum(pieces[k, 48:56, :].astype(F32) for k in range(32)).astype(jnp.int32)
    copy = pltpu.make_async_copy(found, links, sem)
    copy.start()
    for c in range(3):
        held[0:32, :, c * 128 : c * 128 + 128] = pieces[:, c * 16 : c * 16 + 16, :]
    held[32] = jnp.zeros((16, C), BF16)
    copy.wait()

    def body(d, _):
        prv, nxt = links[0, d], links[1, d]
        for j in range(4):
            raw_src = jnp.where(j <= g, prv, jnp.where(j >= g + 2, nxt, -1))
            src = jnp.where(raw, raw_src, jnp.where(j >= g, nxt, -1))
            sorted_blocks[d * 4 + j] = held[jnp.where(src < 0, 32, src)]
        return 0

    sends = []
    for part in range(4):
        lax.fori_loop(part * 8, part * 8 + 8, body, 0, unroll=4)
        at = pl.ds(part * 32, 32)
        sends.append(pltpu.make_async_copy(sorted_blocks.at[at], out.at[at], out_sems.at[part]))
        sends[-1].start()
    for send in sends:
        send.wait()


def share_copies(src, dst, sems):
    inner = pl.ds(COLS, CELLS)
    parts = [(pl.ds(0, 5), inner), (8,), (pl.ds(5, 3), inner), (9, inner)]
    return [
        pltpu.make_async_copy(src.at[part], dst.at[part], sems.at[n])
        for n, part in enumerate(parts)
    ]


def own_kernel(
    table, mine, mine_cot, from1, from2, from3, gain, bias, weight, acc_out,
    taps, x, slab, gslab, acc, h, sums, mean, inv_std, ones, sems, save_sems,
):
    start_weights(weight, taps, sems, 0)
    j = lax.axis_index("space")
    ones[...] = group_matrix()
    acc[...] = jnp.zeros_like(acc)
    for shift, part in enumerate((None, from1, from2, from3)):
        holder = lax.rem(j + 4 - shift, 4)

        def rows(t, _, part=part, holder=holder):
            g, r = t // 2, lax.rem(t, 2)
            at = pl.ds((holder * 2 + r) * COLS, COLS)
            if part is None:
                x[g, at, :] = read_row(lambda half: mine[t * 2 + half])
                cot = read_row(lambda half: mine_cot[t * 2 + half])
            else:
                x[g, at, :] = read_row(lambda half: part[raw_block(j, g) + r * 2 + half])
                cot = read_row(lambda half: part[cot_block(j, g) + r * 2 + half])
            store_shifted(gslab, g, holder * 2 + r, cot.astype(F32))
            return 0

        lax.fori_loop(0, 8, rows, 0, unroll=2)
    frame_stats(x, 4, sums, mean, inv_std, ones)

    def normed(g, _):
        norm_silu_frame(
            x, g, mean[pl.ds(g, 1), :], inv_std[pl.ds(g, 1), :],
            gain[0:1, :], bias[0:1, :], slab, g, None,
        )
        return 0

    lax.fori_loop(0, 4, normed, 0)
    wait_weights(weight, taps, sems, 0)
    start_weights(weight, taps, sems, 1)

    def forward(f, _):
        low = jnp.maximum(0, 4 - j - f)
        n = jnp.minimum(2, 7 - j - f) - low + 1
        by_count(conv_taps, slab, f + low - 4 + j, taps.at[0], low, n, acc, f)
        return 0

    lax.fori_loop(0, 5, forward, 0)
    acc[8, 0:8] = mean[...]
    acc[8, 8:16] = inv_std[...]
    acc[8, COLS : COLS + CELLS] = x[j].astype(F32)
    saves = share_copies(acc, acc_out, save_sems)
    saves[0].start()
    saves[1].start()
    wait_weights(weight, taps, sems, 1)

    def backward(f, _):
        low = jnp.maximum(0, f + j - 1)
        by_count(adjoint_taps, gslab, j + f + 2 - low, taps.at[1], low, 3 - low, acc, 5 + f)
        return 0

    lax.fori_loop(0, 3, backward, 0)

    @pl.when(j >= 2)
    def _():
        for n in range(2):
            h[n] = acc[1 + n, COLS : COLS + CELLS, :].astype(BF16)
        frame_stats(h, 2, sums, mean, inv_std, ones)

        def normed1(n, _):
            norm_silu_frame(
                h, n, mean[pl.ds(n, 1), :], inv_std[pl.ds(n, 1), :],
                gain[1:2, :], bias[1:2, :], slab, n, None,
            )
            return 0

        lax.fori_loop(0, 2, normed1, 0)
        by_count(conv_taps, slab, 3 - j, taps.at[1], 4 - j, j - 1, acc, 9, most=2)

    saves[2].start()
    saves[3].start()
    for save in saves:
        save.wait()


def rest_kernel(
    table, recv, acc_in, gain, bias, weight, out,
    taps, x, slab, gslab, acc, share, h, sums, mean, inv_std, ones, sems, load_sems,
):
    start_weights(weight, taps, sems, 0)
    loads = share_copies(acc_in, share, load_sems)
    j = lax.axis_index("space")
    has_prev = (table[0, 3] >= 0).astype(F32)
    ones[...] = group_matrix()

    def rows(t, _):
        g, row = t // 8, lax.rem(t, 8)
        block = (g * 2 + lax.rem(row, 2)) * 2
        x[g, pl.ds(row * COLS, COLS), :] = read_row(lambda half: recv[(block + half) * 4 + row // 2])
        return 0

    def cot_rows(t, _):
        g, row = t // 8, lax.rem(t, 8)
        block = 16 + (g * 2 + lax.rem(row, 2)) * 2
        cot = read_row(lambda half: recv[(block + half) * 4 + row // 2])
        store_shifted(gslab, g, row, cot.astype(F32))
        return 0

    lax.fori_loop(0, 32, rows, 0, unroll=4)
    frame_stats(x, 4, sums, mean, inv_std, ones)
    start_weights(weight, taps, sems, 1)

    def normed(g, _):
        mask = jnp.where(g >= j, has_prev, 1.0)

        @pl.when(g != j - 1)
        def _():
            norm_silu_frame(
                x, g, mean[pl.ds(g, 1), :], inv_std[pl.ds(g, 1), :],
                gain[0:1, :], bias[0:1, :], slab, g, mask,
            )

        return 0

    lax.fori_loop(0, 4, normed, 0)
    def cot_frame(g, _):
        lax.fori_loop(0, 8, lambda r, _: cot_rows(g * 8 + r, 0), 0, unroll=4)
        return 0

    lax.fori_loop(0, j + 1, cot_frame, 0)
    acc[...] = jnp.zeros_like(acc)
    wait_weights(weight, taps, sems, 0)
    for load in loads:
        load.start()

    def forward(f, _):
        prev = f < 4 - j
        low = jnp.where(prev, 0, jnp.maximum(0, 8 - j - f))
        n = jnp.where(prev, jnp.minimum(2, 3 - j - f), 2) - low + 1
        first = jnp.where(prev, j + f, f + low - 8 + j)
        by_count(conv_taps, slab, first, taps.at[0], low, n, acc, f)
        return 0

    lax.fori_loop(0, 5, forward, 0)
    wait_weights(weight, taps, sems, 1)

    def backward(f, _):
        n = jnp.minimum(2, f + j - 2) + 1
        by_count(adjoint_taps, gslab, f - 2 + j, taps.at[1], 0, n, acc, 5 + f)
        return 0

    lax.fori_loop(0, 3, backward, 0)

    for load in loads:
        load.wait()

    def rounded(f, _):
        inner = pl.ds(COLS, CELLS)
        h[f] = (acc[f, inner, :] + share[f, inner, :]).astype(BF16)
        return 0

    lax.fori_loop(0, 5, rounded, 0)
    frame_stats(h, 5, sums, mean, inv_std, ones)
    gain1, bias1 = gain[1:2, :], bias[1:2, :]

    def normed1(f, _):
        mask = jnp.where(j - 2 + f < 0, has_prev, 1.0)
        norm_silu_frame(
            h, f, mean[pl.ds(f, 1), :], inv_std[pl.ds(f, 1), :], gain1, bias1, slab, f, mask
        )
        return 0

    lax.fori_loop(0, jnp.minimum(3, 4 - j), normed1, 0)

    def norm_back():
        sums[...] = jnp.zeros_like(sums)
        for f in range(3):
            n = f + 2
            one, two = norm_back_sums(
                h, n, mean[n : n + 1, :], inv_std[n : n + 1, :], gain1, bias1, acc, 5 + f, share
            )
            sums[f : f + 1, :] = one
            sums[f + 4 : f + 5, :] = two
        sums[...] = group_mean(sums[...], ones[...])
        for f in range(3):
            n = f + 2
            for r in range(ROWS):
                g1 = norm_back_row(
                    h, n, r, mean[n : n + 1, :], inv_std[n : n + 1, :], acc, 5 + f,
                    sums[f : f + 1, :], sums[f + 4 : f + 5, :],
                )
                store_shifted(gslab, f, r, g1)

    by_count(conv_taps, slab, 0, taps.at[1], 0, jnp.minimum(3, 4 - j), acc, 8, norm_back)
    for i in range(4):
        inner = pl.ds(COLS + i * 64, 64)
        out[i, 0] = (acc[8, inner, :] + share[9, inner, :]).astype(BF16)

    adjoint_taps(gslab, 2, taps.at[0], 0, 3, acc, 9)

    m0, i0 = share[8, pl.ds(j, 1), :], share[8, pl.ds(8 + j, 1), :]
    raw_own = share.at[8:9, COLS : COLS + CELLS]
    one, two = norm_back_sums(raw_own, 0, m0, i0, gain[0:1, :], bias[0:1, :], acc, 9, None)
    sums[0:1, :] = one
    sums[1:2, :] = two
    sums[...] = group_mean(sums[...], ones)
    for r in range(8):
        g0 = norm_back_row(raw_own, 0, r, m0, i0, acc, 9, sums[0:1, :], sums[1:2, :])
        out[r // 2, 1, (r % 2) * COLS : (r % 2 + 1) * COLS, :] = g0.astype(BF16)


def per_device(frames, stretch_table, conv_weight, norm_gain, norm_bias, cotangent):
    small = pltpu.CompilerParams(vmem_limit_bytes=8 * 2**20)
    params = pltpu.CompilerParams(vmem_limit_bytes=115 * 2**19)
    weight = conv_weight.reshape(2, 27, C, C)
    mine, mine_cot = frames.reshape(16, 16, C), cotangent.reshape(16, 16, C)
    pieces, *windows = pl.pallas_call(
        prepare_kernel,
        out_shape=[jax.ShapeDtypeStruct((32, 56, 128), BF16)]
        + [jax.ShapeDtypeStruct((28, 16, C), BF16)] * 3,
        in_specs=[SMEM, VMEM, VMEM],
        out_specs=[VMEM] * 4,
        name="prepare",
    )(stretch_table, mine, mine_cot)
    shifted = [
        lax.ppermute(window, "space", [(i, (i + k) % 4) for i in range(4)])
        for k, window in zip((1, 2, 3), windows)
    ]
    spread = lax.all_to_all(pieces, "stretch", 0, 0, tiled=True)
    routed = pl.pallas_call(
        route_kernel,
        out_shape=jax.ShapeDtypeStruct((128, 16, C), BF16),
        in_specs=[VMEM],
        out_specs=HBM,
        scratch_shapes=[
            pltpu.VMEM((33, 16, C), BF16),
            pltpu.VMEM((8, 128), jnp.int32),
            pltpu.SMEM((8, 128), jnp.int32),
            pltpu.VMEM((128, 16, C), BF16),
            pltpu.SemaphoreType.DMA,
            pltpu.SemaphoreType.DMA((4,)),
        ],
        compiler_params=small,
        name="route",
    )(spread)
    recv = lax.all_to_all(routed, ("stretch", "space"), 0, 0, tiled=True)
    acc = pl.pallas_call(
        own_kernel,
        out_shape=jax.ShapeDtypeStruct((32, PADDED, C), F32),
        in_specs=[SMEM] + [VMEM] * 7 + [ANY],
        out_specs=HBM,
        scratch_shapes=[
            pltpu.VMEM((2, 27, C, C), BF16),
            pltpu.VMEM((4, CELLS, C), BF16),
            pltpu.VMEM((4, CELLS, 3 * C), BF16),
            pltpu.VMEM((4, CELLS, 3 * C), BF16),
            pltpu.VMEM((10, PADDED, C), F32),
            pltpu.VMEM((2, CELLS, C), BF16),
            pltpu.VMEM((8, C), F32),
            pltpu.VMEM((8, C), F32),
            pltpu.VMEM((8, C), F32),
            pltpu.VMEM((C, C), BF16),
            pltpu.SemaphoreType.DMA((2, 3)),
            pltpu.SemaphoreType.DMA((4,)),
        ],
        compiler_params=params,
        cost_estimate=pl.CostEstimate(
            flops=1500 * 2 * CELLS * 9 * C * C, bytes_accessed=24 * 2**20, transcendentals=0
        ),
        name="own",
    )(stretch_table, mine, mine_cot, *shifted, norm_gain, norm_bias, weight)
    out = pl.pallas_call(
        rest_kernel,
        out_shape=jax.ShapeDtypeStruct((4, 2, 64, C), BF16),
        in_specs=[SMEM, VMEM, HBM, VMEM, VMEM, ANY],
        out_specs=VMEM,
        scratch_shapes=[
            pltpu.VMEM((2, 27, C, C), BF16),
            pltpu.VMEM((4, CELLS, C), BF16),
            pltpu.VMEM((4, CELLS, 3 * C), BF16),
            pltpu.VMEM((4, CELLS, 3 * C), BF16),
            pltpu.VMEM((10, PADDED, C), F32),
            pltpu.VMEM((10, PADDED, C), F32),
            pltpu.VMEM((5, CELLS, C), BF16),
            pltpu.VMEM((8, C), F32),
            pltpu.VMEM((8, C), F32),
            pltpu.VMEM((8, C), F32),
            pltpu.VMEM((C, C), BF16),
            pltpu.SemaphoreType.DMA((2, 3)),
            pltpu.SemaphoreType.DMA((4,)),
        ],
        compiler_params=pltpu.CompilerParams(vmem_limit_bytes=48 * 2**20),
        cost_estimate=pl.CostEstimate(
            flops=18 * 2 * CELLS * 9 * C * C, bytes_accessed=24 * 2**20, transcendentals=0
        ),
        name="rest",
    )(stretch_table, recv, acc, norm_gain, norm_bias, weight)
    back = lax.all_to_all(out, "space", 0, 0, tiled=True)
    shape = frames.shape
    return back[:, 0].reshape(shape), back[:, 1].reshape(shape)


def solution(mesh):
    in_specs = (
        P("stretch", "space", None, None),
        P("stretch", None),
        P(),
        P(),
        P(),
        P("stretch", "space", None, None),
    )
    out_specs = (P("stretch", "space", None, None), P("stretch", "space", None, None))
    return jax.shard_map(
        per_device, mesh=mesh, in_specs=in_specs, out_specs=out_specs, check_vma=False
    )
```
